32 devices in a mesh: expert: 8 (over z, y), fsdp: 2 (over x), replica: 2 (over core).
Axes of the slice: x: 2, y: 2, z: 4, core: 2. Of those that a mesh axis runs over, the one named last changes fastest.
Arguments:
- out_grad: bfloat16 [4096, 2048], P(('expert', 'fsdp', 'replica')), may hold values from -6 to 6
- hidden_saved: bfloat16 [4096, 8, 768], P(('expert', 'fsdp', 'replica')), may hold values from -6 to 6
- gate_probs: float32 [4096, 8], P(('expert', 'fsdp', 'replica')), may hold values from 0.05 to 0.5
- expert_ids: int32 [4096, 8], P(('expert', 'fsdp', 'replica')), may hold values from 0 to 15, all different within a row; in each aligned block of 128 rows (0 to 127, 128 to 255, ...) at most 128 rows name the same one
- weight_q: bfloat16 [16, 768, 2048], P('expert', 'fsdp'), may hold values from -0.21875 to 0.21875
- weight_exp: int32 [16, 768, 16], P('expert', 'fsdp'), may hold values from -1 to 1
- master: float32 [16, 768, 2048], P('expert', ('fsdp', 'replica')), may hold values from -0.21875 to 0.21875
- moment1: bfloat16 [16, 768, 2048], P('expert', ('fsdp', 'replica')), may hold values from -6 to 6
- moment2: bfloat16 [16, 768, 2048], P('expert', ('fsdp', 'replica')), may hold values from 0.099609375 to 10
Outputs:
- hidden_grad: bfloat16 [4096, 8, 768], P(('expert', 'fsdp', 'replica'))
- gate_grad: float32 [4096, 8], P(('expert', 'fsdp', 'replica'))
- master_new: float32 [16, 768, 2048], P('expert', ('fsdp', 'replica'))
- moment1_new: bfloat16 [16, 768, 2048], P('expert', ('fsdp', 'replica'))
- moment2_new: bfloat16 [16, 768, 2048], P('expert', ('fsdp', 'replica'))
The draws below stay inside these ranges and needn't reach their ends.
Inputs may be any that keep to these rules, and one draw needn't show every extreme that they name: `expert_ids`: each token names 8 different experts; the tokens of one device name any one expert at most 128 times.
All inputs are finite; a program needn't handle non-finite values.
Results may differ from the reference program's by a relative error of at most 0.0051.
Values may be sent and summed in bfloat16 or wider, within the bound.
No kernel may reach another device: no remote copies, remote signals or barrier semaphores. Data moves between devices by JAX's collectives and lax.ppermute only.
A program may use at most 128 MiB of HBM per device.

```python
import math
import jax
import jax.numpy as jnp
import numpy as np
from jax import lax

D = 2048
FF = 768
TOP = 8
QB = 128
TOK_DEV = 128
EXPERTS = 16
TOKENS = 4096
CAP = 128
N_EXPERT = 8
N_FSDP = 2
N_REPLICA = 2


def set_ends(result, stream_key, low, largest):
    shape = result.shape
    spot = [jax.random.randint(jax.random.fold_in(stream_key, axis), (), 0, shape[axis]) for axis in range(len(shape))]
    result = result.at[tuple(spot)].set(low)
    longest = shape.index(max(shape))
    spot[longest] = (spot[longest] + 1) % shape[longest]
    return result.at[tuple(spot)].set(largest)


def block_levels(stream_key, extent, shards, low, largest):
    def one(dim, shards_of):
        steps = jax.random.uniform(jax.random.fold_in(jax.random.fold_in(stream_key, 6), dim), (shards_of,), jnp.float32, low / len(shards), largest / len(shards))
        return jnp.repeat(jnp.exp(steps), extent[dim] // shards_of).reshape((-1,) + (1,) * (len(extent) - dim - 1))

    level = one(*shards[0])
    for cut in shards[1:]:
        level = level * one(*cut)
    return level


def routed_block(own_key, own, number, rows, number_of, top, bound, slope):
    ranking = jax.random.permutation(own_key, number_of)
    heavy_load, common = shares(number_of, rows * top, bound, slope, True), shares(number_of, rows * top, bound, slope, False)
    places = jnp.arange(number_of)

    def named(sizes, turn):
        used = int((sizes > 0).sum())
        fixed = max(1, used // 4)
        moved = fixed + (places - fixed + turn * (used - fixed)) % max(1, number_of - fixed)
        return jnp.zeros((number_of,), jnp.int32).at[ranking[jnp.where(places < fixed, places, moved)]].set(jnp.asarray(sizes, jnp.int32))

    sizes = jnp.where(number % 4 == 0, named(heavy_load, number // 4), named(common, number - number // 4 - 1))
    mixed = jax.random.permutation(jax.random.fold_in(own, 3), number_of)
    giver, taker = mixed[0:number_of // 2 * 2:2], mixed[1:number_of // 2 * 2:2]
    room = jnp.minimum(sizes[giver] - 1, bound - sizes[taker]) // 2
    room = jnp.where((giver == ranking[0]) | (taker == ranking[0]) | (sizes[taker] == 0), 0, jnp.maximum(room, 0))
    moved = jax.random.randint(jax.random.fold_in(own, 4), (number_of // 2,), 0, 1 << 20) % (room + 1)
    sizes = sizes.at[giver].add(-moved).at[taker].add(moved)
    members = jnp.searchsorted(jnp.cumsum(sizes), jnp.arange(rows * top), side="right").astype(jnp.int32)
    listing = members.reshape(top, rows).T
    listing = listing[jax.random.permutation(jax.random.fold_in(own, 1), rows)]
    turn = jax.random.randint(jax.random.fold_in(own, 2), (rows, 1), 0, top)
    return jnp.take_along_axis(listing, (jnp.arange(top)[None, :] + turn) % top, axis=1)


def shares(amount, total, reach, skew, full):
    loads = [(1 << 20) // math.isqrt(standing ** skew) + 1 for standing in range(1, amount + 1)]
    largest = reach if full else min(reach, max(-(-total // amount), total * loads[0] // sum(loads)))
    least = 1 if total - largest >= amount - 1 else 0
    given, spare = [largest] + [least] * (amount - 1), total - largest - least * (amount - 1)
    while spare > 0:
        candidates = [i for i in range(1, amount) if given[i] < largest] or [i for i in range(1, amount) if given[i] < reach]
        mass, budget = sum([loads[i] for i in candidates]), spare
        for i in candidates:
            more = min(reach - given[i], max(1, budget * loads[i] // mass), spare)
            given[i] = given[i] + more
            spare = spare - more
    return np.array(given)


def scatter_about(key, dims, deviation, reach, cuts=(), kind=jnp.bfloat16):
    values = deviation * jax.random.normal(key, dims, jnp.float32)
    if cuts:
        values = values * block_levels(key, dims, cuts, -0.22, 0.18)
    return jnp.clip(values, -reach, reach).astype(kind)


def setup_inputs(seed: int = 0) -> dict:
    key_list = jax.random.split(jax.random.key(seed), 10)
    out_grad = scatter_about(key_list[0], (TOKENS, D), 1.0, 6.0, ((0, 32),))
    hidden_saved = scatter_about(key_list[1], (TOKENS, TOP, FF), 1.0, 6.0, ((0, 32),))
    gate_probs = jnp.clip(jnp.exp(math.log(0.5) - 2.3025851 * jax.random.uniform(key_list[2], (TOKENS, TOP), jnp.float32) ** block_levels(key_list[2], (TOKENS, TOP), ((0, 32),), -0.2, 0.2)), 0.05, 0.5)
    expert_ids_keys = jax.random.split(jax.random.fold_in(key_list[3], 1), TOKENS // TOK_DEV)
    expert_ids_turns = jax.random.permutation(jax.random.fold_in(key_list[3], 3), TOKENS // TOK_DEV)
    expert_ids = jax.vmap(lambda own, number: routed_block(jax.random.fold_in(key_list[3], 2), own, number, TOK_DEV, EXPERTS, TOP, CAP, 2))(expert_ids_keys, expert_ids_turns).reshape((TOKENS, TOP))
    weight_q = scatter_about(key_list[4], (EXPERTS, FF, D), FF ** -0.5, 0.21875, ((0, 8), (1, 2)))
    weight_exp = set_ends(jax.random.randint(key_list[5], (EXPERTS, FF, D // QB), -1, 2), jax.random.fold_in(key_list[5], 1), -1, 1).astype(jnp.int32)
    master = scatter_about(key_list[6], (EXPERTS, FF, D), FF ** -0.5, 0.21875, ((0, 8), (1, 4)), jnp.float32)
    moment1 = scatter_about(key_list[7], (EXPERTS, FF, D), 1.0, 6.0, ((0, 8), (1, 4)))
    moment2 = jnp.clip(jnp.exp(math.log(10.0) - 4.609084 * jax.random.uniform(key_list[8], (EXPERTS, FF, D), jnp.float32) ** block_levels(key_list[8], (EXPERTS, FF, D), ((0, 8), (1, 4)), -0.2, 0.2)), 0.099609375, 10.0).astype(jnp.bfloat16)
    return dict(out_grad=out_grad, hidden_saved=hidden_saved, gate_probs=gate_probs, expert_ids=expert_ids, weight_q=weight_q, weight_exp=weight_exp, master=master, moment1=moment1, moment2=moment2)


def reference(out_grad, hidden_saved, gate_probs, expert_ids, weight_q, weight_exp, master, moment1, moment2):
    scales = jnp.exp2(weight_exp.astype(jnp.float32))
    weight = (weight_q.astype(jnp.float32).reshape(EXPERTS, FF, D // QB, QB) * scales[..., None]).reshape(EXPERTS, FF, D).astype(jnp.bfloat16)
    routes = TOKENS * TOP
    weighted = (gate_probs[..., None] * hidden_saved.astype(jnp.float32)).astype(jnp.bfloat16).reshape(routes, FF)
    flat_ids = expert_ids.reshape(-1).astype(jnp.int32)
    sorted_routes = jnp.argsort(flat_ids, stable=True).astype(jnp.int32)
    counts = jnp.bincount(flat_ids, length=EXPERTS).astype(jnp.int32)
    starts = (jnp.cumsum(counts) - counts).astype(jnp.int32)
    max_rows = N_EXPERT * N_FSDP * N_REPLICA * CAP
    padded = jnp.concatenate([sorted_routes, jnp.zeros((max_rows,), jnp.int32)])

    def per_expert(index):
        chosen = lax.dynamic_slice_in_dim(padded, starts[index], max_rows)
        is_valid = jnp.arange(max_rows) < counts[index]
        dy_rows = jnp.where(is_valid[:, None], out_grad[chosen // TOP], jnp.zeros((), jnp.bfloat16))
        h_rows = jnp.where(is_valid[:, None], weighted[chosen], jnp.zeros((), jnp.bfloat16))
        back_rows = jnp.dot(dy_rows, weight[index].T, preferred_element_type=jnp.float32).astype(jnp.bfloat16)
        part_grad = jnp.dot(h_rows.T, dy_rows, preferred_element_type=jnp.float32)
        return (back_rows, part_grad)
    backs, gradient = lax.map(per_expert, jnp.arange(EXPERTS, dtype=jnp.int32))
    position = jnp.zeros((routes,), jnp.int32).at[sorted_routes].set(jnp.arange(routes, dtype=jnp.int32))
    local_pos = position - starts[flat_ids]
    back_route = backs.reshape(EXPERTS * max_rows, FF)[flat_ids * max_rows + local_pos].reshape(TOKENS, TOP, FF)
    back_float = back_route.astype(jnp.float32)
    hidden_grad = (gate_probs[..., None] * back_float).astype(jnp.bfloat16)
    gate_grad = lax.optimization_barrier(jnp.sum(hidden_saved.astype(jnp.float32) * back_float, axis=-1))
    first = 0.9 * moment1.astype(jnp.float32) + 0.1 * gradient
    second = 0.95 * moment2.astype(jnp.float32) + 0.05 * gradient * gradient
    update = first / (1.0 - 0.9 ** 20) / (jnp.sqrt(second / (1.0 - 0.95 ** 20)) + 1e-08) + 0.1 * master
    master_new = master - 0.001 * update
    return (hidden_grad, gate_grad, master_new, first.astype(jnp.bfloat16), second.astype(jnp.bfloat16))
```

```python
import jax
import jax.numpy as jnp
from jax import lax
from jax.experimental import pallas as pl
from jax.experimental.pallas import tpu as pltpu
from jax.sharding import PartitionSpec as P

def slots_body(
    out_grad, hidden_saved, gate_probs, expert_ids, weight_q, weight_exp, master, moment1, moment2
):
    tokens_here, top_count = expert_ids.shape
    experts_here, rows_here, model_width = weight_q.shape
    hidden_width = hidden_saved.shape[2]
    expert_groups = lax.axis_size("expert")
    experts_all = expert_groups * experts_here
    capacity = min(tokens_here, 2 * tokens_here * top_count // experts_all)
    routes = tokens_here * top_count
    flat_ids = expert_ids.reshape(-1)
    onehot = (flat_ids[:, None] == jnp.arange(experts_all, dtype=jnp.int32)[None, :]).astype(
        jnp.int32
    )
    rank_in_expert = jnp.sum(jnp.cumsum(onehot, axis=0) * onehot, axis=1) - 1
    slot_index = flat_ids * capacity + rank_in_expert
    route_of_slot = (
        jnp.full((experts_all * capacity,), routes, jnp.int32)
        .at[slot_index]
        .set(jnp.arange(routes, dtype=jnp.int32))
    )
    filled = route_of_slot < routes
    clamped = jnp.minimum(route_of_slot, routes - 1)
    weighted = (
        (gate_probs[..., None] * hidden_saved.astype(jnp.float32))
        .astype(jnp.bfloat16)
        .reshape(routes, hidden_width)
    )
    zero_value = jnp.zeros((), jnp.bfloat16)
    dy_send = jnp.where(filled[:, None], out_grad[clamped // top_count], zero_value)
    weighted_send = jnp.where(filled[:, None], weighted[clamped], zero_value)
    dy_send = dy_send.reshape(expert_groups, experts_here, capacity, model_width)
    weighted_send = weighted_send.reshape(expert_groups, experts_here, capacity, hidden_width)
    recv_dy, recv_weighted = (
        lax.all_to_all(dy_send, "expert", split_axis=0, concat_axis=0, tiled=True),
        lax.all_to_all(weighted_send, "expert", split_axis=0, concat_axis=0, tiled=True),
    )
    scales = jnp.exp2(weight_exp.astype(jnp.float32))
    blocks = weight_exp.shape[2]
    weight_local = (
        (
            weight_q.astype(jnp.float32).reshape(
                experts_here, rows_here, blocks, model_width // blocks
            )
            * scales[..., None]
        )
        .reshape(experts_here, rows_here, model_width)
        .astype(jnp.bfloat16)
    )
    back_rows = jnp.einsum(
        "secd,efd->secf",
        recv_dy,
        lax.all_gather(weight_local, "fsdp", axis=1, tiled=True),
        preferred_element_type=jnp.float32,
    ).astype(jnp.bfloat16)
    returned = lax.all_to_all(back_rows, "expert", split_axis=0, concat_axis=0, tiled=True)
    back_route = returned.reshape(experts_all * capacity, hidden_width)[slot_index].reshape(
        tokens_here, top_count, hidden_width
    )
    back_float = back_route.astype(jnp.float32)
    hidden_grad = (gate_probs[..., None] * back_float).astype(jnp.bfloat16)
    gate_grad = jnp.sum(hidden_saved.astype(jnp.float32) * back_float, axis=-1)
    partial_grad = jnp.einsum(
        "secf,secd->efd", recv_weighted, recv_dy, preferred_element_type=jnp.float32
    )
    gradient = lax.psum_scatter(partial_grad, ("fsdp", "replica"), scatter_dimension=1, tiled=True)
    first = 0.9 * moment1.astype(jnp.float32) + 0.1 * gradient
    second = 0.95 * moment2.astype(jnp.float32) + 0.05 * gradient * gradient
    update = first / (1.0 - 0.9**20) / (jnp.sqrt(second / (1.0 - 0.95**20)) + 1e-08) + 0.1 * master
    master_new = master - 0.001 * update
    return (
        hidden_grad,
        gate_grad,
        master_new,
        first.astype(jnp.bfloat16),
        second.astype(jnp.bfloat16),
    )


VMEM = 100 * 2**20 // 2
TOKEN_BLOCK = 16


def pick(index, options):
    result = options[0]
    for number, option in enumerate(options[1:], 1):
        result = jnp.where(index == number, option, result)
    return result


def route_match(ids, column_keys):
    tokens, top = ids.shape
    shape = (tokens, top, top)
    token = lax.broadcasted_iota(jnp.int32, shape, 0)
    diagonal = lax.broadcasted_iota(jnp.int32, shape, 1) == lax.broadcasted_iota(
        jnp.int32, shape, 2
    )
    keys = jnp.where(diagonal, ids[:, None, :] * tokens + token, 0).astype(jnp.float32)
    keys = jnp.sum(keys.reshape(tokens * top, top), axis=1, keepdims=True)
    return jnp.where(keys == column_keys, 1.0, 0.0).astype(jnp.bfloat16)


def route_column(values):
    tokens, top = values.shape
    shape = (tokens, top, top)
    diagonal = lax.broadcasted_iota(jnp.int32, shape, 1) == lax.broadcasted_iota(
        jnp.int32, shape, 2
    )
    spread = jnp.where(diagonal, jnp.broadcast_to(values[:, None, :], shape), 0.0)
    return jnp.sum(spread.reshape(tokens * top, top), axis=1, keepdims=True)


def route_square(column, tokens, top):
    shape = (tokens, top, top)
    diagonal = lax.broadcasted_iota(jnp.int32, shape, 1) == lax.broadcasted_iota(
        jnp.int32, shape, 2
    )
    spread = jnp.broadcast_to(column, (tokens * top, top)).reshape(shape)
    return jnp.sum(jnp.where(diagonal, spread, 0.0), axis=1)


def spread_kernel(groups, here, parts, place, keys, ids, gate, hidden, *outs):
    fsdp, replica = parts
    tokens, top, width = hidden.shape
    unit = width // (fsdp * replica)
    match = route_match(ids[...], keys[...])
    values = hidden[...].astype(jnp.float32).reshape(tokens * top, width)
    weighted = (route_column(gate[...]) * values).astype(jnp.bfloat16)

    def block(f, r):
        at = (f * replica + r) * unit
        return weighted[:, at : at + unit]

    shares = [
        pick(
            place[1],
            [
                jnp.concatenate([block((f + o) % fsdp, r) for o in range(fsdp)], axis=1)
                for f in range(fsdp)
            ],
        )
        for r in range(replica)
    ]
    for c in range(replica):
        share = pick(place[2], [shares[(r + c) % replica] for r in range(replica)])
        rows = lax.dot_general(
            match, share, (((0,), (0,)), ((), ())), preferred_element_type=jnp.float32
        ).astype(jnp.bfloat16)
        for g in range(groups):
            for e in range(here):
                at = (g * here + e) * tokens
                outs[g * replica + c][:, e * fsdp * unit : (e + 1) * fsdp * unit] = rows[
                    at : at + tokens
                ]


def collect_kernel(groups, here, parts, place, keys, ids, gate, hidden, *refs):
    fsdp, replica = parts
    backs, (hidden_grad, gate_grad) = refs[:-2], refs[-2:]
    tokens, top, width = hidden.shape
    unit = width // (fsdp * replica)
    match = route_match(ids[...], keys[...])
    found = []
    for c in range(replica):
        rows = jnp.concatenate(
            [
                backs[g * replica + c][:, e * fsdp * unit : (e + 1) * fsdp * unit]
                for g in range(groups)
                for e in range(here)
            ],
            axis=0,
        )
        found.append(jnp.dot(match, rows, preferred_element_type=jnp.float32))
    shares = [
        pick(place[2], [found[(h - r) % replica] for r in range(replica)])
        for h in range(replica)
    ]
    back = jnp.concatenate(
        [
            pick(
                place[1],
                [
                    shares[h][:, (f - m) % fsdp * unit : ((f - m) % fsdp + 1) * unit]
                    for m in range(fsdp)
                ],
            )
            for f in range(fsdp)
            for h in range(replica)
        ],
        axis=1,
    )
    values = hidden[...].astype(jnp.float32).reshape(tokens * top, width)
    scaled = route_column(gate[...]) * back
    hidden_grad[...] = scaled.reshape(tokens, top, width).astype(jnp.bfloat16)
    gate_grad[...] = route_square(jnp.sum(values * back, axis=1, keepdims=True), tokens, top)


def scale_kernel(place, values, exponents, out):
    blocks = exponents.shape[2]
    width = values.shape[2] // blocks
    scales = jnp.exp2(exponents[0].astype(jnp.float32))
    for b in range(blocks):
        at = slice(b * width, (b + 1) * width)
        out[0, :, at] = (values[0, :, at].astype(jnp.float32) * scales[:, b : b + 1]).astype(
            jnp.bfloat16
        )


def dense_body(
    out_grad, hidden_saved, gate_probs, expert_ids, weight_q, weight_exp, master, moment1, moment2
):
    tokens, top = expert_ids.shape
    here, rows_here, model_width = weight_q.shape
    width = hidden_saved.shape[2]
    groups = lax.axis_size("expert")
    fsdp, replica = lax.axis_size("fsdp"), lax.axis_size("replica")
    me, mf, mr = lax.axis_index("expert"), lax.axis_index("fsdp"), lax.axis_index("replica")
    inner = 2 if groups % 2 == 0 else 1
    outer = groups // inner
    unit = width // (fsdp * replica)
    block = min(TOKEN_BLOCK, tokens)
    offsets = [(s, j) for s in range(outer) for j in range(inner)]

    def moved(e, s, j):
        return (e // inner + s) % outer * inner + (e % inner + j) % inner

    def send(x, s, j, c):
        if (s, j, c) == (0, 0, 0):
            return x
        pairs = [
            (e * replica + r, moved(e, s, j) * replica + (r + c) % replica)
            for e in range(groups)
            for r in range(replica)
        ]
        return lax.ppermute(x, ("expert", "replica"), pairs)

    place = jnp.stack([me, mf, mr]).astype(jnp.int32)
    weight_part = pl.pallas_call(
        scale_kernel,
        out_shape=jax.ShapeDtypeStruct((here, unit, model_width), jnp.bfloat16),
        grid_spec=pltpu.PrefetchScalarGridSpec(
            num_scalar_prefetch=1,
            grid=(here,),
            in_specs=[
                pl.BlockSpec((1, unit, model_width), lambda e, p: (e, p[2], 0)),
                pl.BlockSpec((1, unit, weight_exp.shape[2]), lambda e, p: (e, p[2], 0)),
            ],
            out_specs=pl.BlockSpec((1, unit, model_width), lambda e, p: (e, 0, 0)),
        ),
        compiler_params=pltpu.CompilerParams(vmem_limit_bytes=VMEM),
        name="scale",
    )(place, weight_q, weight_exp)

    ups = outer // 2
    line = {0: out_grad}
    for s in range(1, ups + 1):
        line[s] = send(line[s - 1], 1, 0, 0)
    for s in range(outer - 1, ups, -1):
        line[s] = send(line[(s + 1) % outer], outer - 1, 0, 0)
    dy = {}
    for s in range(outer):
        for j in range(inner):
            held = send(line[s], 0, j, 0)
            for c in range(replica):
                dy[s, j, c] = send(held, 0, 0, c)

    weight_parts = [weight_part] + [
        lax.ppermute(weight_part, "fsdp", [(f, (f - o) % fsdp) for f in range(fsdp)])
        for o in range(1, fsdp)
    ]
    weight_rows = jnp.stack(weight_parts, axis=1).reshape(here * fsdp * unit, model_width)

    def keys(sign):
        group = [
            ((me // inner + sign * s) % outer) * inner + (me % inner + sign * j) % inner
            for s, j in offsets
        ]
        expert = (jnp.stack(group)[:, None] * here + jnp.arange(here)[None, :]).reshape(-1)
        return (
            (expert[:, None] * block + jnp.arange(block)[None, :])
            .reshape(1, -1)
            .astype(jnp.float32)
        )

    column_keys = keys(1)
    pieces = len(offsets) * replica
    piece = (here * fsdp * unit,)
    row_spec = pl.BlockSpec((block,) + piece, lambda i, p: (i, 0))
    token_specs = [
        pl.BlockSpec(column_keys.shape, lambda i, p: (0, 0)),
        pl.BlockSpec((block, top), lambda i, p: (i, 0)),
        pl.BlockSpec((block, top), lambda i, p: (i, 0)),
        pl.BlockSpec((block, top, width), lambda i, p: (i, 0, 0)),
    ]
    spread = pl.pallas_call(
        lambda *refs: spread_kernel(groups, here, (fsdp, replica), *refs),
        out_shape=[jax.ShapeDtypeStruct((tokens,) + piece, jnp.bfloat16)] * pieces,
        grid_spec=pltpu.PrefetchScalarGridSpec(
            num_scalar_prefetch=1,
            grid=(tokens // block,),
            in_specs=token_specs,
            out_specs=[row_spec] * pieces,
        ),
        compiler_params=pltpu.CompilerParams(vmem_limit_bytes=VMEM),
        name="spread",
    )(place, column_keys, expert_ids, gate_probs, hidden_saved)
    spread, _ = lax.optimization_barrier((spread, line[ups]))
    order = [(s, j, c) for s, j in offsets for c in range(replica)]
    hid = {o: send(x, *o) for o, x in zip(order, spread)}

    back = [
        lax.dot_general(
            dy[o], weight_rows, (((1,), (1,)), ((), ())), preferred_element_type=jnp.float32
        ).astype(jnp.bfloat16)
        for o in order
    ]
    back, hid = lax.optimization_barrier((back, hid))
    returned = [
        send(x, (-s) % outer, (-j) % inner, (-c) % replica) for (s, j, c), x in zip(order, back)
    ]

    hid_all = jnp.concatenate([hid[o] for o in order], axis=0)
    dy_all = jnp.concatenate([dy[o] for o in order], axis=0)
    partial_grad = lax.dot_general(
        hid_all, dy_all, (((0,), (0,)), ((), ())), preferred_element_type=jnp.float32
    ).reshape(here, fsdp, unit, model_width)
    gradient = partial_grad[:, 0]
    for o in range(1, fsdp):
        gradient = gradient + lax.ppermute(
            partial_grad[:, o].astype(jnp.bfloat16),
            "fsdp",
            [(f, (f + o) % fsdp) for f in range(fsdp)],
        ).astype(jnp.float32)
    first = 0.9 * moment1.astype(jnp.float32) + 0.1 * gradient
    second = 0.95 * moment2.astype(jnp.float32) + 0.05 * gradient * gradient
    update = first / (1.0 - 0.9**20) / (jnp.sqrt(second / (1.0 - 0.95**20)) + 1e-08) + 0.1 * master
    master_new = master - 0.001 * update

    hidden_grad, gate_grad = pl.pallas_call(
        lambda *refs: collect_kernel(groups, here, (fsdp, replica), *refs),
        out_shape=[
            jax.ShapeDtypeStruct(hidden_saved.shape, jnp.bfloat16),
            jax.ShapeDtypeStruct(gate_probs.shape, jnp.float32),
        ],
        grid_spec=pltpu.PrefetchScalarGridSpec(
            num_scalar_prefetch=1,
            grid=(tokens // block,),
            in_specs=token_specs + [row_spec] * pieces,
            out_specs=[
                pl.BlockSpec((block, top, width), lambda i, p: (i, 0, 0)),
                pl.BlockSpec((block, top), lambda i, p: (i, 0)),
            ],
        ),
        compiler_params=pltpu.CompilerParams(vmem_limit_bytes=VMEM),
        name="collect",
    )(place, column_keys, expert_ids, gate_probs, hidden_saved, *returned)
    return (
        hidden_grad,
        gate_grad,
        master_new,
        first.astype(jnp.bfloat16),
        second.astype(jnp.bfloat16),
    )


def body(*args):
    tokens, top = args[3].shape
    experts = lax.axis_size("expert") * args[4].shape[0]
    if min(tokens, 2 * tokens * top // experts) == tokens:
        return dense_body(*args)
    return slots_body(*args)


def solution(mesh):
    in_specs = (
        P(("expert", "fsdp", "replica"), None),
        P(("expert", "fsdp", "replica"), None, None),
        P(("expert", "fsdp", "replica"), None),
        P(("expert", "fsdp", "replica"), None),
        P("expert", "fsdp", None),
        P("expert", "fsdp", None),
        P("expert", ("fsdp", "replica"), None),
        P("expert", ("fsdp", "replica"), None),
        P("expert", ("fsdp", "replica"), None),
    )
    out_specs = (
        P(("expert", "fsdp", "replica"), None, None),
        P(("expert", "fsdp", "replica"), None),
        P("expert", ("fsdp", "replica"), None),
        P("expert", ("fsdp", "replica"), None),
        P("expert", ("fsdp", "replica"), None),
    )
    return jax.shard_map(body, mesh=mesh, in_specs=in_specs, out_specs=out_specs, check_vma=False)
```

```python
import jax
import jax.numpy as jnp
from jax import lax
from jax.experimental import pallas as pl
from jax.experimental.pallas import tpu as pltpu
from jax.sharding import PartitionSpec as P

def slots_body(
    out_grad, hidden_saved, gate_probs, expert_ids, weight_q, weight_exp, master, moment1, moment2
):
    tokens_here, top_count = expert_ids.shape
    experts_here, rows_here, model_width = weight_q.shape
    hidden_width = hidden_saved.shape[2]
    expert_groups = lax.axis_size("expert")
    experts_all = expert_groups * experts_here
    capacity = min(tokens_here, 2 * tokens_here * top_count // experts_all)
    routes = tokens_here * top_count
    flat_ids = expert_ids.reshape(-1)
    onehot = (flat_ids[:, None] == jnp.arange(experts_all, dtype=jnp.int32)[None, :]).astype(
        jnp.int32
    )
    rank_in_expert = jnp.sum(jnp.cumsum(onehot, axis=0) * onehot, axis=1) - 1
    slot_index = flat_ids * capacity + rank_in_expert
    route_of_slot = (
        jnp.full((experts_all * capacity,), routes, jnp.int32)
        .at[slot_index]
        .set(jnp.arange(routes, dtype=jnp.int32))
    )
    filled = route_of_slot < routes
    clamped = jnp.minimum(route_of_slot, routes - 1)
    weighted = (
        (gate_probs[..., None] * hidden_saved.astype(jnp.float32))
        .astype(jnp.bfloat16)
        .reshape(routes, hidden_width)
    )
    zero_value = jnp.zeros((), jnp.bfloat16)
    dy_send = jnp.where(filled[:, None], out_grad[clamped // top_count], zero_value)
    weighted_send = jnp.where(filled[:, None], weighted[clamped], zero_value)
    dy_send = dy_send.reshape(expert_groups, experts_here, capacity, model_width)
    weighted_send = weighted_send.reshape(expert_groups, experts_here, capacity, hidden_width)
    recv_dy, recv_weighted = (
        lax.all_to_all(dy_send, "expert", split_axis=0, concat_axis=0, tiled=True),
        lax.all_to_all(weighted_send, "expert", split_axis=0, concat_axis=0, tiled=True),
    )
    scales = jnp.exp2(weight_exp.astype(jnp.float32))
    blocks = weight_exp.shape[2]
    weight_local = (
        (
            weight_q.astype(jnp.float32).reshape(
                experts_here, rows_here, blocks, model_width // blocks
            )
            * scales[..., None]
        )
        .reshape(experts_here, rows_here, model_width)
        .astype(jnp.bfloat16)
    )
    back_rows = jnp.einsum(
        "secd,efd->secf",
        recv_dy,
        lax.all_gather(weight_local, "fsdp", axis=1, tiled=True),
        preferred_element_type=jnp.float32,
    ).astype(jnp.bfloat16)
    returned = lax.all_to_all(back_rows, "expert", split_axis=0, concat_axis=0, tiled=True)
    back_route = returned.reshape(experts_all * capacity, hidden_width)[slot_index].reshape(
        tokens_here, top_count, hidden_width
    )
    back_float = back_route.astype(jnp.float32)
    hidden_grad = (gate_probs[..., None] * back_float).astype(jnp.bfloat16)
    gate_grad = jnp.sum(hidden_saved.astype(jnp.float32) * back_float, axis=-1)
    partial_grad = jnp.einsum(
        "secf,secd->efd", recv_weighted, recv_dy, preferred_element_type=jnp.float32
    )
    gradient = lax.psum_scatter(partial_grad, ("fsdp", "replica"), scatter_dimension=1, tiled=True)
    first = 0.9 * moment1.astype(jnp.float32) + 0.1 * gradient
    second = 0.95 * moment2.astype(jnp.float32) + 0.05 * gradient * gradient
    update = first / (1.0 - 0.9**20) / (jnp.sqrt(second / (1.0 - 0.95**20)) + 1e-08) + 0.1 * master
    master_new = master - 0.001 * update
    return (
        hidden_grad,
        gate_grad,
        master_new,
        first.astype(jnp.bfloat16),
        second.astype(jnp.bfloat16),
    )


VMEM = 100 * 2**20 // 2
TOKEN_BLOCK = 16


def pick(index, options):
    result = options[0]
    for number, option in enumerate(options[1:], 1):
        result = jnp.where(index == number, option, result)
    return result


def route_match(ids, experts):
    tokens, top = ids.shape
    shape = (tokens, top, top)
    token = lax.broadcasted_iota(jnp.int32, shape, 0)
    diagonal = lax.broadcasted_iota(jnp.int32, shape, 1) == lax.broadcasted_iota(
        jnp.int32, shape, 2
    )
    keys = jnp.where(diagonal, ids[:, None, :] * tokens + token, 0).astype(jnp.float32)
    keys = jnp.sum(keys.reshape(tokens * top, top), axis=1, keepdims=True).astype(jnp.int32)
    columns = lax.broadcasted_iota(jnp.int32, (tokens * top, experts * tokens), 1)
    return jnp.where(keys == columns, 1.0, 0.0).astype(jnp.bfloat16)


def route_column(values):
    tokens, top = values.shape
    shape = (tokens, top, top)
    diagonal = lax.broadcasted_iota(jnp.int32, shape, 1) == lax.broadcasted_iota(
        jnp.int32, shape, 2
    )
    spread = jnp.where(diagonal, jnp.broadcast_to(values[:, None, :], shape), 0.0)
    return jnp.sum(spread.reshape(tokens * top, top), axis=1, keepdims=True)


def route_square(column, tokens, top):
    shape = (tokens, top, top)
    diagonal = lax.broadcasted_iota(jnp.int32, shape, 1) == lax.broadcasted_iota(
        jnp.int32, shape, 2
    )
    spread = jnp.broadcast_to(column, (tokens * top, top)).reshape(shape)
    return jnp.sum(jnp.where(diagonal, spread, 0.0), axis=1)


def spread_kernel(here, parts, place, ids, gate, hidden, out):
    fsdp, replica = parts
    tokens, top, width = hidden.shape
    groups = out.shape[1]
    unit = width // (fsdp * replica)
    match = route_match(ids[...], groups * here)
    values = hidden[...].astype(jnp.float32).reshape(tokens * top, width)
    weighted = (route_column(gate[...]) * values).astype(jnp.bfloat16)

    def block(f, r):
        at = (f * replica + r) * unit
        return weighted[:, at : at + unit]

    for r in range(replica):
        share = pick(
            place[1],
            [
                jnp.concatenate([block((f + o) % fsdp, r) for o in range(fsdp)], axis=1)
                for f in range(fsdp)
            ],
        )
        rows = lax.dot_general(
            match, share, (((0,), (0,)), ((), ())), preferred_element_type=jnp.float32
        ).astype(jnp.bfloat16)
        for g in range(groups):
            for e in range(here):
                at = (g * here + e) * tokens
                out[r, g, :, e * fsdp * unit : (e + 1) * fsdp * unit] = rows[at : at + tokens]


def collect_kernel(here, parts, ids, gate, hidden, backs, hidden_grad, gate_grad):
    fsdp, replica = parts
    tokens, top, width = hidden.shape
    groups = backs.shape[1]
    unit = width // (fsdp * replica)
    match = route_match(ids[...], groups * here)
    shares = []
    for r in range(replica):
        rows = jnp.concatenate(
            [
                backs[r, g, :, e * fsdp * unit : (e + 1) * fsdp * unit]
                for g in range(groups)
                for e in range(here)
            ],
            axis=0,
        )
        shares.append(jnp.dot(match, rows, preferred_element_type=jnp.float32))
    back = jnp.concatenate(
        [
            shares[r][:, f * unit : (f + 1) * unit]
            for f in range(fsdp)
            for r in range(replica)
        ],
        axis=1,
    )
    values = hidden[...].astype(jnp.float32).reshape(tokens * top, width)
    scaled = route_column(gate[...]) * back
    hidden_grad[...] = scaled.reshape(tokens, top, width).astype(jnp.bfloat16)
    gate_grad[...] = route_square(jnp.sum(values * back, axis=1, keepdims=True), tokens, top)


def scale_kernel(place, values, exponents, out):
    blocks = exponents.shape[2]
    width = values.shape[2] // blocks
    scales = jnp.exp2(exponents[0].astype(jnp.float32))
    for b in range(blocks):
        at = slice(b * width, (b + 1) * width)
        out[0, :, at] = (values[0, :, at].astype(jnp.float32) * scales[:, b : b + 1]).astype(
            jnp.bfloat16
        )


def back_kernel(parts, place, dy, *refs):
    fsdp = parts[0]
    weights, out, rows = refs[:fsdp], refs[-2], refs[-1]
    here, unit, _ = weights[0].shape

    @pl.when(pl.program_id(0) == 0)
    def _():
        for e in range(here):
            for o in range(fsdp):
                at = (e * fsdp + lax.rem(place[1] + o, fsdp)) * unit
                rows[pl.ds(pl.multiple_of(at, unit), unit), :] = weights[o][e]

    back = lax.dot_general(
        dy[...], rows[...], (((1,), (1,)), ((), ())), preferred_element_type=jnp.float32
    )
    out[...] = back.astype(jnp.bfloat16).reshape(out.shape)


def gradient_kernel(parts, place, *refs):
    fsdp, replica = parts
    hids, dys, outs, turned = (
        refs[:replica],
        refs[replica : 2 * replica],
        refs[2 * replica : -1],
        refs[-1],
    )
    here, unit, _ = outs[0].shape

    @pl.when(pl.program_id(0) == 0)
    def _():
        for c in range(replica):
            turned[c] = hids[c][...].reshape(turned.shape[2], turned.shape[1]).T

    total = sum(
        jnp.dot(turned[c], dys[c][...], preferred_element_type=jnp.float32)
        for c in range(replica)
    )
    for e in range(here):
        for o in range(fsdp):
            at = (e * fsdp + o) * unit
            outs[o][e] = total[at : at + unit].astype(outs[o].dtype)


def dense_body(
    out_grad, hidden_saved, gate_probs, expert_ids, weight_q, weight_exp, master, moment1, moment2
):
    tokens, top = expert_ids.shape
    here, rows_here, model_width = weight_q.shape
    width = hidden_saved.shape[2]
    groups = lax.axis_size("expert")
    fsdp, replica = lax.axis_size("fsdp"), lax.axis_size("replica")
    me, mf, mr = lax.axis_index("expert"), lax.axis_index("fsdp"), lax.axis_index("replica")
    inner = 2 if groups % 2 == 0 else 1
    outer = groups // inner
    unit = width // (fsdp * replica)
    block = min(TOKEN_BLOCK, tokens)
    lanes = here * fsdp * unit

    def moved(e, s, j):
        return (e // inner + s) % outer * inner + (e % inner + j) % inner

    def send(x, s, j):
        return lax.ppermute(x, "expert", [(e, moved(e, s, j)) for e in range(groups)])

    def exchange(x):
        x = x.reshape(replica * groups, tokens, lanes)
        x = lax.all_to_all(x, ("replica", "expert"), split_axis=0, concat_axis=0, tiled=True)
        return x.reshape(replica, groups, tokens, lanes)

    place = jnp.stack([me, mf, mr]).astype(jnp.int32)
    weight_part = pl.pallas_call(
        scale_kernel,
        out_shape=jax.ShapeDtypeStruct((here, unit, model_width), jnp.bfloat16),
        grid_spec=pltpu.PrefetchScalarGridSpec(
            num_scalar_prefetch=1,
            grid=(here,),
            in_specs=[
                pl.BlockSpec((1, unit, model_width), lambda e, p: (e, p[2], 0)),
                pl.BlockSpec((1, unit, weight_exp.shape[2]), lambda e, p: (e, p[2], 0)),
            ],
            out_specs=pl.BlockSpec((1, unit, model_width), lambda e, p: (e, 0, 0)),
        ),
        compiler_params=pltpu.CompilerParams(vmem_limit_bytes=VMEM),
        name="scale",
    )(place, weight_q, weight_exp)

    token_specs = [
        pl.BlockSpec((block, top), lambda i, p: (i, 0)),
        pl.BlockSpec((block, top), lambda i, p: (i, 0)),
        pl.BlockSpec((block, top, width), lambda i, p: (i, 0, 0)),
    ]
    row_spec = pl.BlockSpec((replica, groups, block, lanes), lambda i, p: (0, 0, i, 0))
    spread = pl.pallas_call(
        lambda *refs: spread_kernel(here, (fsdp, replica), *refs),
        out_shape=jax.ShapeDtypeStruct((replica, groups, tokens, lanes), jnp.bfloat16),
        grid_spec=pltpu.PrefetchScalarGridSpec(
            num_scalar_prefetch=1,
            grid=(tokens // block,),
            in_specs=token_specs,
            out_specs=row_spec,
        ),
        compiler_params=pltpu.CompilerParams(vmem_limit_bytes=VMEM),
        name="spread",
    )(place, expert_ids, gate_probs, hidden_saved)

    ups = outer // 2
    line = {0: out_grad}
    for s in range(1, ups + 1):
        line[s] = send(line[s - 1], 1, 0)
        if s == 1:
            line[1], spread, weight_part = lax.optimization_barrier((line[1], spread, weight_part))
    for s in range(outer - 1, ups, -1):
        line[s] = send(line[(s + 1) % outer], outer - 1, 0)
    hid = exchange(spread)
    weight_parts = [weight_part] + [
        lax.ppermute(weight_part, "fsdp", [(f, (f - o) % fsdp) for f in range(fsdp)])
        for o in range(1, fsdp)
    ]
    line[ups], weight_parts = lax.optimization_barrier((line[ups], weight_parts))
    own = jnp.zeros((groups, tokens, model_width), jnp.bfloat16)
    for s in range(outer):
        for j in range(inner):
            piece = send(line[s], 0, j) if j else line[s]
            source = lax.rem(lax.div(me, inner) + (outer - s), outer) * inner + lax.rem(
                me + (inner - j), inner
            )
            own = lax.dynamic_update_index_in_dim(own, piece, source, 0)
    own = own.reshape(groups * tokens, model_width)
    dy = [own] + [
        lax.ppermute(own, "replica", [(r, (r - c) % replica) for r in range(replica)])
        for c in range(1, replica)
    ]

    together = 2 if groups % 2 == 0 else 1
    part_spec = pl.BlockSpec((here, unit, model_width), lambda i, p: (0, 0, 0))
    back = []
    for c in range(replica):
        back = [
            pl.pallas_call(
                lambda *refs: back_kernel((fsdp, replica), *refs),
                out_shape=jax.ShapeDtypeStruct((replica, groups, tokens, lanes), jnp.bfloat16),
                grid_spec=pltpu.PrefetchScalarGridSpec(
                    num_scalar_prefetch=1,
                    grid=(groups // together,),
                    in_specs=[
                        pl.BlockSpec((together * tokens, model_width), lambda i, p: (i, 0))
                    ]
                    + [part_spec] * fsdp
                    + [pl.BlockSpec(memory_space=pl.ANY)] * len(back),
                    out_specs=pl.BlockSpec(
                        (1, together, tokens, lanes),
                        lambda i, p, c=c: (lax.rem(p[2] + c, replica), i, 0, 0),
                    ),
                    scratch_shapes=[pltpu.VMEM((lanes, model_width), jnp.bfloat16)],
                ),
                compiler_params=pltpu.CompilerParams(vmem_limit_bytes=VMEM),
                cost_estimate=pl.CostEstimate(
                    flops=2 * groups * tokens * lanes * model_width,
                    bytes_accessed=2 * groups * tokens * (lanes + model_width),
                    transcendentals=0,
                ),
                input_output_aliases={2 + fsdp: 0} if back else {},
                name="back",
            )(place, dy[c], *weight_parts, *back)
        ]
    back, hid = lax.optimization_barrier((back[0], hid))
    returned = exchange(back)

    columns = min(512, model_width)
    grad_spec = pl.BlockSpec((here, unit, columns), lambda i, p: (0, 0, i))
    grads = pl.pallas_call(
        lambda *refs: gradient_kernel((fsdp, replica), *refs),
        out_shape=[
            jax.ShapeDtypeStruct((here, unit, model_width), jnp.bfloat16 if o else jnp.float32)
            for o in range(fsdp)
        ],
        grid_spec=pltpu.PrefetchScalarGridSpec(
            num_scalar_prefetch=1,
            grid=(model_width // columns,),
            in_specs=[
                pl.BlockSpec(
                    (1, groups, tokens, lanes),
                    lambda i, p, c=c: (lax.rem(p[2] + c, replica), 0, 0, 0),
                )
                for c in range(replica)
            ]
            + [pl.BlockSpec((groups * tokens, columns), lambda i, p: (0, i))] * replica,
            out_specs=[grad_spec] * fsdp,
            scratch_shapes=[pltpu.VMEM((replica, lanes, groups * tokens), jnp.bfloat16)],
        ),
        compiler_params=pltpu.CompilerParams(vmem_limit_bytes=VMEM),
        cost_estimate=pl.CostEstimate(
            flops=2 * replica * groups * tokens * lanes * model_width,
            bytes_accessed=2 * replica * groups * tokens * (lanes + model_width),
            transcendentals=0,
        ),
        name="gradient",
    )(place, *[hid] * replica, *dy)
    gradient = grads[0]
    for o in range(1, fsdp):
        gradient = gradient + lax.ppermute(
            grads[o], "fsdp", [(f, (f + o) % fsdp) for f in range(fsdp)]
        ).astype(jnp.float32)
    first = 0.9 * moment1.astype(jnp.float32) + 0.1 * gradient
    second = 0.95 * moment2.astype(jnp.float32) + 0.05 * gradient * gradient
    update = first / (1.0 - 0.9**20) / (jnp.sqrt(second / (1.0 - 0.95**20)) + 1e-08) + 0.1 * master
    master_new = master - 0.001 * update

    new = (master_new, first.astype(jnp.bfloat16), second.astype(jnp.bfloat16))
    returned, new = lax.optimization_barrier((returned, new))
    hidden_grad, gate_grad = pl.pallas_call(
        lambda *refs: collect_kernel(here, (fsdp, replica), *refs),
        out_shape=[
            jax.ShapeDtypeStruct(hidden_saved.shape, jnp.bfloat16),
            jax.ShapeDtypeStruct(gate_probs.shape, jnp.float32),
        ],
        grid=(tokens // block,),
        in_specs=[
            pl.BlockSpec((block, top), lambda i: (i, 0)),
            pl.BlockSpec((block, top), lambda i: (i, 0)),
            pl.BlockSpec((block, top, width), lambda i: (i, 0, 0)),
            pl.BlockSpec((replica, groups, block, lanes), lambda i: (0, 0, i, 0)),
        ],
        out_specs=[
            pl.BlockSpec((block, top, width), lambda i: (i, 0, 0)),
            pl.BlockSpec((block, top), lambda i: (i, 0)),
        ],
        compiler_params=pltpu.CompilerParams(vmem_limit_bytes=VMEM),
        name="collect",
    )(expert_ids, gate_probs, hidden_saved, returned)
    return (hidden_grad, gate_grad) + new


def body(*args):
    tokens, top = args[3].shape
    experts = lax.axis_size("expert") * args[4].shape[0]
    if min(tokens, 2 * tokens * top // experts) == tokens:
        return dense_body(*args)
    return slots_body(*args)


def solution(mesh):
    in_specs = (
        P(("expert", "fsdp", "replica"), None),
        P(("expert", "fsdp", "replica"), None, None),
        P(("expert", "fsdp", "replica"), None),
        P(("expert", "fsdp", "replica"), None),
        P("expert", "fsdp", None),
        P("expert", "fsdp", None),
        P("expert", ("fsdp", "replica"), None),
        P("expert", ("fsdp", "replica"), None),
        P("expert", ("fsdp", "replica"), None),
    )
    out_specs = (
        P(("expert", "fsdp", "replica"), None, None),
        P(("expert", "fsdp", "replica"), None),
        P("expert", ("fsdp", "replica"), None),
        P("expert", ("fsdp", "replica"), None),
        P("expert", ("fsdp", "replica"), None),
    )
    return jax.shard_map(body, mesh=mesh, in_specs=in_specs, out_specs=out_specs, check_vma=False)
```

```python
import jax
import jax.numpy as jnp
from jax import lax
from jax.experimental import pallas as pl
from jax.experimental.pallas import tpu as pltpu
from jax.sharding import PartitionSpec as P

def slots_body(
    out_grad, hidden_saved, gate_probs, expert_ids, weight_q, weight_exp, master, moment1, moment2
):
    tokens_here, top_count = expert_ids.shape
    experts_here, rows_here, model_width = weight_q.shape
    hidden_width = hidden_saved.shape[2]
    expert_groups = lax.axis_size("expert")
    experts_all = expert_groups * experts_here
    capacity = min(tokens_here, 2 * tokens_here * top_count // experts_all)
    routes = tokens_here * top_count
    flat_ids = expert_ids.reshape(-1)
    onehot = (flat_ids[:, None] == jnp.arange(experts_all, dtype=jnp.int32)[None, :]).astype(
        jnp.int32
    )
    rank_in_expert = jnp.sum(jnp.cumsum(onehot, axis=0) * onehot, axis=1) - 1
    slot_index = flat_ids * capacity + rank_in_expert
    route_of_slot = (
        jnp.full((experts_all * capacity,), routes, jnp.int32)
        .at[slot_index]
        .set(jnp.arange(routes, dtype=jnp.int32))
    )
    filled = route_of_slot < routes
    clamped = jnp.minimum(route_of_slot, routes - 1)
    weighted = (
        (gate_probs[..., None] * hidden_saved.astype(jnp.float32))
        .astype(jnp.bfloat16)
        .reshape(routes, hidden_width)
    )
    zero_value = jnp.zeros((), jnp.bfloat16)
    dy_send = jnp.where(filled[:, None], out_grad[clamped // top_count], zero_value)
    weighted_send = jnp.where(filled[:, None], weighted[clamped], zero_value)
    dy_send = dy_send.reshape(expert_groups, experts_here, capacity, model_width)
    weighted_send = weighted_send.reshape(expert_groups, experts_here, capacity, hidden_width)
    recv_dy, recv_weighted = (
        lax.all_to_all(dy_send, "expert", split_axis=0, concat_axis=0, tiled=True),
        lax.all_to_all(weighted_send, "expert", split_axis=0, concat_axis=0, tiled=True),
    )
    scales = jnp.exp2(weight_exp.astype(jnp.float32))
    blocks = weight_exp.shape[2]
    weight_local = (
        (
            weight_q.astype(jnp.float32).reshape(
                experts_here, rows_here, blocks, model_width // blocks
            )
            * scales[..., None]
        )
        .reshape(experts_here, rows_here, model_width)
        .astype(jnp.bfloat16)
    )
    back_rows = jnp.einsum(
        "secd,efd->secf",
        recv_dy,
        lax.all_gather(weight_local, "fsdp", axis=1, tiled=True),
        preferred_element_type=jnp.float32,
    ).astype(jnp.bfloat16)
    returned = lax.all_to_all(back_rows, "expert", split_axis=0, concat_axis=0, tiled=True)
    back_route = returned.reshape(experts_all * capacity, hidden_width)[slot_index].reshape(
        tokens_here, top_count, hidden_width
    )
    back_float = back_route.astype(jnp.float32)
    hidden_grad = (gate_probs[..., None] * back_float).astype(jnp.bfloat16)
    gate_grad = jnp.sum(hidden_saved.astype(jnp.float32) * back_float, axis=-1)
    partial_grad = jnp.einsum(
        "secf,secd->efd", recv_weighted, recv_dy, preferred_element_type=jnp.float32
    )
    gradient = lax.psum_scatter(partial_grad, ("fsdp", "replica"), scatter_dimension=1, tiled=True)
    first = 0.9 * moment1.astype(jnp.float32) + 0.1 * gradient
    second = 0.95 * moment2.astype(jnp.float32) + 0.05 * gradient * gradient
    update = first / (1.0 - 0.9**20) / (jnp.sqrt(second / (1.0 - 0.95**20)) + 1e-08) + 0.1 * master
    master_new = master - 0.001 * update
    return (
        hidden_grad,
        gate_grad,
        master_new,
        first.astype(jnp.bfloat16),
        second.astype(jnp.bfloat16),
    )


VMEM = 100 * 2**20 // 2
TOKEN_BLOCK = 16
PARTS = 4


def pick(index, options):
    result = options[0]
    for number, option in enumerate(options[1:], 1):
        result = jnp.where(index == number, option, result)
    return result


def diagonal(shape):
    return lax.broadcasted_iota(jnp.int32, shape, 1) == lax.broadcasted_iota(jnp.int32, shape, 2)


def route_column(values):
    tokens, top = values.shape
    shape = (tokens, top, top)
    spread = jnp.where(diagonal(shape), jnp.broadcast_to(values[:, None, :], shape), 0.0)
    return jnp.sum(spread.reshape(tokens * top, top), axis=1, keepdims=True)


def route_square(column, tokens, top):
    shape = (tokens, top, top)
    spread = jnp.broadcast_to(column, (tokens * top, top)).reshape(shape)
    return jnp.sum(jnp.where(diagonal(shape), spread, 0.0), axis=1)


def route_match(ids, experts):
    tokens, top = ids.shape
    token = lax.broadcasted_iota(jnp.int32, (tokens, top), 0).astype(jnp.float32)
    keys = route_column(ids * tokens + token).astype(jnp.int32)
    columns = lax.broadcasted_iota(jnp.int32, (tokens * top, experts * tokens), 1)
    return jnp.where(keys == columns, 1.0, 0.0).astype(jnp.bfloat16)


def turn_routes(ids, gate, turned):
    @pl.when(pl.program_id(0) == 0)
    def _():
        turned[0] = ids[...].astype(jnp.float32).T
        turned[1] = gate[...].T


def rows_of_part(step, part, tokens):
    start = pl.program_id(0) * step + part * tokens
    return pl.ds(pl.multiple_of(start, tokens), tokens)


def spread_kernel(here, parts, place, ids, gate, hidden, out, turned):
    fsdp, replica = parts
    step, top, width = hidden.shape
    tokens = min(TOKEN_BLOCK, step)
    groups = out.shape[1]
    unit = width // (fsdp * replica)
    turn_routes(ids, gate, turned)
    for part in range(step // tokens):
        inside = slice(part * tokens, (part + 1) * tokens)
        at = rows_of_part(step, part, tokens)
        match = route_match(turned[0, at], groups * here)
        values = hidden[inside].astype(jnp.float32).reshape(tokens * top, width)
        weighted = (route_column(turned[1, at]) * values).astype(jnp.bfloat16)
        for r in range(replica):
            blocks = [
                weighted[:, (f * replica + r) * unit : (f * replica + r + 1) * unit]
                for f in range(fsdp)
            ]
            share = pick(
                place[1],
                [jnp.concatenate(blocks[f:] + blocks[:f], axis=1) for f in range(fsdp)],
            )
            rows = lax.dot_general(
                match, share, (((0,), (0,)), ((), ())), preferred_element_type=jnp.float32
            ).astype(jnp.bfloat16)
            for g in range(groups):
                for e in range(here):
                    row = (g * here + e) * tokens
                    out[r, g, inside, e * fsdp * unit : (e + 1) * fsdp * unit] = rows[
                        row : row + tokens
                    ]


def collect_kernel(
    here, parts, ids, gate, hidden, backs, hidden_grad, gate_grad, turned, gate_turned
):
    fsdp, replica = parts
    step, top, width = hidden.shape
    tokens = min(TOKEN_BLOCK, step)
    groups = backs.shape[1]
    unit = width // (fsdp * replica)
    turn_routes(ids, gate, turned)
    for part in range(step // tokens):
        inside = slice(part * tokens, (part + 1) * tokens)
        at = rows_of_part(step, part, tokens)
        match = route_match(turned[0, at], groups * here)
        shares = []
        for r in range(replica):
            rows = jnp.concatenate(
                [
                    backs[r, g, inside, e * fsdp * unit : (e + 1) * fsdp * unit]
                    for g in range(groups)
                    for e in range(here)
                ],
                axis=0,
            )
            shares.append(jnp.dot(match, rows, preferred_element_type=jnp.float32))
        back = jnp.concatenate(
            [
                shares[r][:, f * unit : (f + 1) * unit]
                for f in range(fsdp)
                for r in range(replica)
            ],
            axis=1,
        )
        values = hidden[inside].astype(jnp.float32).reshape(tokens * top, width)
        scaled = route_column(turned[1, at]) * back
        hidden_grad[inside] = scaled.reshape(tokens, top, width).astype(jnp.bfloat16)
        column = jnp.sum(values * back, axis=1, keepdims=True)
        gate_turned[at] = route_square(column, tokens, top)

    @pl.when(pl.program_id(0) == pl.num_programs(0) - 1)
    def _():
        gate_grad[...] = gate_turned[...].T


def scale_kernel(place, values, exponents, out, scales):
    _, unit, model_width = values.shape
    blocks = exponents.shape[1]
    width = model_width // blocks
    scales[...] = jnp.exp2(exponents[0].astype(jnp.float32)).T
    rows = scales[pl.ds(pl.multiple_of(place[2] * unit, unit), unit), :]
    for b in range(blocks):
        at = slice(b * width, (b + 1) * width)
        out[0, :, at] = (values[0, :, at].astype(jnp.float32) * rows[:, b : b + 1]).astype(
            jnp.bfloat16
        )


def back_kernel(parts, place, dy, *refs):
    fsdp = parts[0]
    weights, out, rows = refs[:fsdp], refs[-2], refs[-1]
    here, unit, _ = weights[0].shape

    @pl.when(pl.program_id(0) == 0)
    def _():
        for e in range(here):
            for o in range(fsdp):
                at = (e * fsdp + lax.rem(place[1] + o, fsdp)) * unit
                rows[pl.ds(pl.multiple_of(at, unit), unit), :] = weights[o][e]

    back = lax.dot_general(
        dy[...], rows[...], (((1,), (1,)), ((), ())), preferred_element_type=jnp.float32
    )
    out[...] = back.astype(jnp.bfloat16).reshape(out.shape)


def gradient_kernel(parts, place, *refs):
    fsdp, replica = parts
    hids, dys, outs, turned = (
        refs[:replica],
        refs[replica : 2 * replica],
        refs[2 * replica : -1],
        refs[-1],
    )
    here, unit, _ = outs[0].shape

    @pl.when(pl.program_id(0) == 0)
    def _():
        for c in range(replica):
            turned[c] = hids[c][...].reshape(turned.shape[2], turned.shape[1]).T

    total = sum(
        jnp.dot(turned[c], dys[c][...], preferred_element_type=jnp.float32)
        for c in range(replica)
    )
    for e in range(here):
        for o in range(fsdp):
            at = (e * fsdp + o) * unit
            outs[o][e] = total[at : at + unit].astype(outs[o].dtype)


def dense_body(
    out_grad, hidden_saved, gate_probs, expert_ids, weight_q, weight_exp, master, moment1, moment2
):
    tokens, top = expert_ids.shape
    here, rows_here, model_width = weight_q.shape
    width = hidden_saved.shape[2]
    groups = lax.axis_size("expert")
    fsdp, replica = lax.axis_size("fsdp"), lax.axis_size("replica")
    me, mf, mr = lax.axis_index("expert"), lax.axis_index("fsdp"), lax.axis_index("replica")
    inner = 2 if groups % 2 == 0 else 1
    outer = groups // inner
    unit = width // (fsdp * replica)
    block = min(TOKEN_BLOCK * PARTS, tokens)
    lanes = here * fsdp * unit

    def moved(e, s, j):
        return (e // inner + s) % outer * inner + (e % inner + j) % inner

    def send(x, s, j):
        return lax.ppermute(x, "expert", [(e, moved(e, s, j)) for e in range(groups)])

    def exchange(x):
        x = x.reshape(replica * groups, tokens, lanes)
        x = lax.all_to_all(x, ("replica", "expert"), split_axis=0, concat_axis=0, tiled=True)
        return x.reshape(replica, groups, tokens, lanes)

    place = jnp.stack([me, mf, mr]).astype(jnp.int32)
    weight_part = pl.pallas_call(
        scale_kernel,
        out_shape=jax.ShapeDtypeStruct((here, unit, model_width), jnp.bfloat16),
        grid_spec=pltpu.PrefetchScalarGridSpec(
            num_scalar_prefetch=1,
            grid=(here,),
            in_specs=[
                pl.BlockSpec((1, unit, model_width), lambda e, p: (e, p[2], 0)),
                pl.BlockSpec((1, weight_exp.shape[2], rows_here), lambda e, p: (e, 0, 0)),
            ],
            out_specs=pl.BlockSpec((1, unit, model_width), lambda e, p: (e, 0, 0)),
            scratch_shapes=[pltpu.VMEM((rows_here, weight_exp.shape[2]), jnp.float32)],
        ),
        compiler_params=pltpu.CompilerParams(vmem_limit_bytes=VMEM),
        name="scale",
    )(place, weight_q, weight_exp.swapaxes(1, 2))

    token_specs = [
        pl.BlockSpec((top, tokens), lambda i, p: (0, 0)),
        pl.BlockSpec((top, tokens), lambda i, p: (0, 0)),
        pl.BlockSpec((block, top, width), lambda i, p: (i, 0, 0)),
    ]
    turned = pltpu.VMEM((2, tokens, top), jnp.float32)
    row_spec = pl.BlockSpec((replica, groups, block, lanes), lambda i, p: (0, 0, i, 0))
    spread = pl.pallas_call(
        lambda *refs: spread_kernel(here, (fsdp, replica), *refs),
        out_shape=jax.ShapeDtypeStruct((replica, groups, tokens, lanes), jnp.bfloat16),
        grid_spec=pltpu.PrefetchScalarGridSpec(
            num_scalar_prefetch=1,
            grid=(tokens // block,),
            in_specs=token_specs,
            out_specs=row_spec,
            scratch_shapes=[turned],
        ),
        compiler_params=pltpu.CompilerParams(vmem_limit_bytes=VMEM),
        name="spread",
    )(place, expert_ids.T, gate_probs.T, hidden_saved)

    ups = outer // 2
    line = {0: out_grad}
    pair = {}
    if outer > 1:
        line[1] = send(out_grad, 1, 0)
    if outer > 2:
        line[outer - 1] = send(out_grad, outer - 1, 0)
    if inner > 1:
        pair[0] = send(out_grad, 0, 1)
    line, pair, spread = lax.optimization_barrier((line, pair, spread))
    hid = exchange(spread)
    for s in range(2, ups + 1):
        line[s] = send(line[s - 1], 1, 0)
    for s in range(outer - 2, ups, -1):
        line[s] = send(line[s + 1], outer - 1, 0)
    weight_parts = [weight_part] + [
        lax.ppermute(weight_part, "fsdp", [(f, (f - o) % fsdp) for f in range(fsdp)])
        for o in range(1, fsdp)
    ]
    own = jnp.zeros((groups, tokens, model_width), jnp.bfloat16)
    for s in range(outer):
        for j in range(inner):
            piece = line[s]
            if j:
                piece = pair[s] if s in pair else send(line[s], 0, j)
            source = lax.rem(lax.div(me, inner) + (outer - s), outer) * inner + lax.rem(
                me + (inner - j), inner
            )
            own = lax.dynamic_update_index_in_dim(own, piece, source, 0)
    own, weight_parts = lax.optimization_barrier(
        (own.reshape(groups * tokens, model_width), weight_parts)
    )
    dy = [own] + [
        lax.ppermute(own, "replica", [(r, (r - c) % replica) for r in range(replica)])
        for c in range(1, replica)
    ]

    together = max(g for g in (1, 2, 4) if groups % g == 0)
    part_spec = pl.BlockSpec((here, unit, model_width), lambda i, p: (0, 0, 0))
    back = []
    for c in range(replica):
        back = [
            pl.pallas_call(
                lambda *refs: back_kernel((fsdp, replica), *refs),
                out_shape=jax.ShapeDtypeStruct((replica, groups, tokens, lanes), jnp.bfloat16),
                grid_spec=pltpu.PrefetchScalarGridSpec(
                    num_scalar_prefetch=1,
                    grid=(groups // together,),
                    in_specs=[
                        pl.BlockSpec((together * tokens, model_width), lambda i, p: (i, 0))
                    ]
                    + [part_spec] * fsdp
                    + [pl.BlockSpec(memory_space=pl.ANY)] * len(back),
                    out_specs=pl.BlockSpec(
                        (1, together, tokens, lanes),
                        lambda i, p, c=c: (lax.rem(p[2] + c, replica), i, 0, 0),
                    ),
                    scratch_shapes=[pltpu.VMEM((lanes, model_width), jnp.bfloat16)],
                ),
                compiler_params=pltpu.CompilerParams(vmem_limit_bytes=VMEM),
                cost_estimate=pl.CostEstimate(
                    flops=2 * groups * tokens * lanes * model_width,
                    bytes_accessed=2 * groups * tokens * (lanes + model_width),
                    transcendentals=0,
                ),
                input_output_aliases={2 + fsdp: 0} if back else {},
                name="back",
            )(place, dy[c], *weight_parts, *back)
        ]
    back, hid = lax.optimization_barrier((back[0], hid))
    returned = exchange(back)

    columns = min(512, model_width)
    grad_spec = pl.BlockSpec((here, unit, columns), lambda i, p: (0, 0, i))
    grads = pl.pallas_call(
        lambda *refs: gradient_kernel((fsdp, replica), *refs),
        out_shape=[
            jax.ShapeDtypeStruct((here, unit, model_width), jnp.bfloat16 if o else jnp.float32)
            for o in range(fsdp)
        ],
        grid_spec=pltpu.PrefetchScalarGridSpec(
            num_scalar_prefetch=1,
            grid=(model_width // columns,),
            in_specs=[
                pl.BlockSpec(
                    (1, groups, tokens, lanes),
                    lambda i, p, c=c: (lax.rem(p[2] + c, replica), 0, 0, 0),
                )
                for c in range(replica)
            ]
            + [pl.BlockSpec((groups * tokens, columns), lambda i, p: (0, i))] * replica,
            out_specs=[grad_spec] * fsdp,
            scratch_shapes=[pltpu.VMEM((replica, lanes, groups * tokens), jnp.bfloat16)],
        ),
        compiler_params=pltpu.CompilerParams(vmem_limit_bytes=VMEM),
        cost_estimate=pl.CostEstimate(
            flops=2 * replica * groups * tokens * lanes * model_width,
            bytes_accessed=2 * replica * groups * tokens * (lanes + model_width),
            transcendentals=0,
        ),
        name="gradient",
    )(place, *[hid] * replica, *dy)
    gradient = grads[0]
    for o in range(1, fsdp):
        gradient = gradient + lax.ppermute(
            grads[o], "fsdp", [(f, (f + o) % fsdp) for f in range(fsdp)]
        ).astype(jnp.float32)
    first = 0.9 * moment1.astype(jnp.float32) + 0.1 * gradient
    second = 0.95 * moment2.astype(jnp.float32) + 0.05 * gradient * gradient
    update = first / (1.0 - 0.9**20) / (jnp.sqrt(second / (1.0 - 0.95**20)) + 1e-08) + 0.1 * master
    master_new = master - 0.001 * update

    new = (master_new, first.astype(jnp.bfloat16), second.astype(jnp.bfloat16))
    returned, new = lax.optimization_barrier((returned, new))
    hidden_grad, gate_grad = pl.pallas_call(
        lambda *refs: collect_kernel(here, (fsdp, replica), *refs),
        out_shape=[
            jax.ShapeDtypeStruct(hidden_saved.shape, jnp.bfloat16),
            jax.ShapeDtypeStruct((top, tokens), jnp.float32),
        ],
        grid=(tokens // block,),
        in_specs=[
            pl.BlockSpec((top, tokens), lambda i: (0, 0)),
            pl.BlockSpec((top, tokens), lambda i: (0, 0)),
            pl.BlockSpec((block, top, width), lambda i: (i, 0, 0)),
            pl.BlockSpec((replica, groups, block, lanes), lambda i: (0, 0, i, 0)),
        ],
        out_specs=[
            pl.BlockSpec((block, top, width), lambda i: (i, 0, 0)),
            pl.BlockSpec((top, tokens), lambda i: (0, 0)),
        ],
        scratch_shapes=[turned, pltpu.VMEM((tokens, top), jnp.float32)],
        compiler_params=pltpu.CompilerParams(vmem_limit_bytes=VMEM),
        name="collect",
    )(expert_ids.T, gate_probs.T, hidden_saved, returned)
    return (hidden_grad, gate_grad.T) + new


def body(*args):
    tokens, top = args[3].shape
    experts = lax.axis_size("expert") * args[4].shape[0]
    if min(tokens, 2 * tokens * top // experts) == tokens:
        return dense_body(*args)
    return slots_body(*args)


def solution(mesh):
    in_specs = (
        P(("expert", "fsdp", "replica"), None),
        P(("expert", "fsdp", "replica"), None, None),
        P(("expert", "fsdp", "replica"), None),
        P(("expert", "fsdp", "replica"), None),
        P("expert", "fsdp", None),
        P("expert", "fsdp", None),
        P("expert", ("fsdp", "replica"), None),
        P("expert", ("fsdp", "replica"), None),
        P("expert", ("fsdp", "replica"), None),
    )
    out_specs = (
        P(("expert", "fsdp", "replica"), None, None),
        P(("expert", "fsdp", "replica"), None),
        P("expert", ("fsdp", "replica"), None),
        P("expert", ("fsdp", "replica"), None),
        P("expert", ("fsdp", "replica"), None),
    )
    return jax.shard_map(body, mesh=mesh, in_specs=in_specs, out_specs=out_specs, check_vma=False)
```

```python
import jax
import jax.numpy as jnp
from jax import lax
from jax.experimental import pallas as pl
from jax.experimental.pallas import tpu as pltpu
from jax.sharding import PartitionSpec as P

def slots_body(
    out_grad, hidden_saved, gate_probs, expert_ids, weight_q, weight_exp, master, moment1, moment2
):
    tokens_here, top_count = expert_ids.shape
    experts_here, rows_here, model_width = weight_q.shape
    hidden_width = hidden_saved.shape[2]
    expert_groups = lax.axis_size("expert")
    experts_all = expert_groups * experts_here
    capacity = min(tokens_here, 2 * tokens_here * top_count // experts_all)
    routes = tokens_here * top_count
    flat_ids = expert_ids.reshape(-1)
    onehot = (flat_ids[:, None] == jnp.arange(experts_all, dtype=jnp.int32)[None, :]).astype(
        jnp.int32
    )
    rank_in_expert = jnp.sum(jnp.cumsum(onehot, axis=0) * onehot, axis=1) - 1
    slot_index = flat_ids * capacity + rank_in_expert
    route_of_slot = (
        jnp.full((experts_all * capacity,), routes, jnp.int32)
        .at[slot_index]
        .set(jnp.arange(routes, dtype=jnp.int32))
    )
    filled = route_of_slot < routes
    clamped = jnp.minimum(route_of_slot, routes - 1)
    weighted = (
        (gate_probs[..., None] * hidden_saved.astype(jnp.float32))
        .astype(jnp.bfloat16)
        .reshape(routes, hidden_width)
    )
    zero_value = jnp.zeros((), jnp.bfloat16)
    dy_send = jnp.where(filled[:, None], out_grad[clamped // top_count], zero_value)
    weighted_send = jnp.where(filled[:, None], weighted[clamped], zero_value)
    dy_send = dy_send.reshape(expert_groups, experts_here, capacity, model_width)
    weighted_send = weighted_send.reshape(expert_groups, experts_here, capacity, hidden_width)
    recv_dy, recv_weighted = (
        lax.all_to_all(dy_send, "expert", split_axis=0, concat_axis=0, tiled=True),
        lax.all_to_all(weighted_send, "expert", split_axis=0, concat_axis=0, tiled=True),
    )
    scales = jnp.exp2(weight_exp.astype(jnp.float32))
    blocks = weight_exp.shape[2]
    weight_local = (
        (
            weight_q.astype(jnp.float32).reshape(
                experts_here, rows_here, blocks, model_width // blocks
            )
            * scales[..., None]
        )
        .reshape(experts_here, rows_here, model_width)
        .astype(jnp.bfloat16)
    )
    back_rows = jnp.einsum(
        "secd,efd->secf",
        recv_dy,
        lax.all_gather(weight_local, "fsdp", axis=1, tiled=True),
        preferred_element_type=jnp.float32,
    ).astype(jnp.bfloat16)
    returned = lax.all_to_all(back_rows, "expert", split_axis=0, concat_axis=0, tiled=True)
    back_route = returned.reshape(experts_all * capacity, hidden_width)[slot_index].reshape(
        tokens_here, top_count, hidden_width
    )
    back_float = back_route.astype(jnp.float32)
    hidden_grad = (gate_probs[..., None] * back_float).astype(jnp.bfloat16)
    gate_grad = jnp.sum(hidden_saved.astype(jnp.float32) * back_float, axis=-1)
    partial_grad = jnp.einsum(
        "secf,secd->efd", recv_weighted, recv_dy, preferred_element_type=jnp.float32
    )
    gradient = lax.psum_scatter(partial_grad, ("fsdp", "replica"), scatter_dimension=1, tiled=True)
    first = 0.9 * moment1.astype(jnp.float32) + 0.1 * gradient
    second = 0.95 * moment2.astype(jnp.float32) + 0.05 * gradient * gradient
    update = first / (1.0 - 0.9**20) / (jnp.sqrt(second / (1.0 - 0.95**20)) + 1e-08) + 0.1 * master
    master_new = master - 0.001 * update
    return (
        hidden_grad,
        gate_grad,
        master_new,
        first.astype(jnp.bfloat16),
        second.astype(jnp.bfloat16),
    )


VMEM = 100 * 2**20 // 2
TOKEN_BLOCK = 16
PARTS = 4


def pick(index, options):
    result = options[0]
    for number, option in enumerate(options[1:], 1):
        result = jnp.where(index == number, option, result)
    return result


def diagonal(shape):
    return lax.broadcasted_iota(jnp.int32, shape, 1) == lax.broadcasted_iota(jnp.int32, shape, 2)


def route_column(values):
    tokens, top = values.shape
    shape = (tokens, top, top)
    spread = jnp.where(diagonal(shape), jnp.broadcast_to(values[:, None, :], shape), 0.0)
    return jnp.sum(spread.reshape(tokens * top, top), axis=1, keepdims=True)


def route_square(column, tokens, top):
    shape = (tokens, top, top)
    spread = jnp.broadcast_to(column, (tokens * top, top)).reshape(shape)
    return jnp.sum(jnp.where(diagonal(shape), spread, 0.0), axis=1)


def route_match(ids, experts):
    tokens, top = ids.shape
    token = lax.broadcasted_iota(jnp.int32, (tokens, top), 0).astype(jnp.float32)
    keys = route_column(ids * tokens + token).astype(jnp.int32)
    columns = lax.broadcasted_iota(jnp.int32, (tokens * top, experts * tokens), 1)
    return jnp.where(keys == columns, 1.0, 0.0).astype(jnp.bfloat16)


def turn_routes(ids, gate, turned):
    @pl.when(pl.program_id(0) == 0)
    def _():
        turned[0] = ids[...].astype(jnp.float32).T
        turned[1] = gate[...].T


def rows_of_part(step, part, tokens):
    start = pl.program_id(0) * step + part * tokens
    return pl.ds(pl.multiple_of(start, tokens), tokens)


def spread_kernel(here, parts, place, ids, gate, hidden, out, turned):
    fsdp, replica = parts
    step, top, width = hidden.shape
    tokens = min(TOKEN_BLOCK, step)
    groups = out.shape[1]
    unit = width // (fsdp * replica)
    turn_routes(ids, gate, turned)
    for part in range(step // tokens):
        inside = slice(part * tokens, (part + 1) * tokens)
        at = rows_of_part(step, part, tokens)
        match = route_match(turned[0, at], groups * here)
        values = hidden[inside].astype(jnp.float32).reshape(tokens * top, width)
        weighted = (route_column(turned[1, at]) * values).astype(jnp.bfloat16)
        for r in range(replica):
            blocks = [
                weighted[:, (f * replica + r) * unit : (f * replica + r + 1) * unit]
                for f in range(fsdp)
            ]
            share = pick(
                place[1],
                [jnp.concatenate(blocks[f:] + blocks[:f], axis=1) for f in range(fsdp)],
            )
            rows = lax.dot_general(
                match, share, (((0,), (0,)), ((), ())), preferred_element_type=jnp.float32
            ).astype(jnp.bfloat16)
            for g in range(groups):
                for e in range(here):
                    row = (g * here + e) * tokens
                    out[r, g, inside, e * fsdp * unit : (e + 1) * fsdp * unit] = rows[
                        row : row + tokens
                    ]


def collect_kernel(
    here, parts, ids, gate, hidden, backs, hidden_grad, gate_grad, turned, gate_turned
):
    fsdp, replica = parts
    step, top, width = hidden.shape
    tokens = min(TOKEN_BLOCK, step)
    groups = backs.shape[1]
    unit = width // (fsdp * replica)
    turn_routes(ids, gate, turned)
    for part in range(step // tokens):
        inside = slice(part * tokens, (part + 1) * tokens)
        at = rows_of_part(step, part, tokens)
        match = route_match(turned[0, at], groups * here)
        shares = []
        for r in range(replica):
            rows = jnp.concatenate(
                [
                    backs[r, g, inside, e * fsdp * unit : (e + 1) * fsdp * unit]
                    for g in range(groups)
                    for e in range(here)
                ],
                axis=0,
            )
            shares.append(jnp.dot(match, rows, preferred_element_type=jnp.float32))
        back = jnp.concatenate(
            [
                shares[r][:, f * unit : (f + 1) * unit]
                for f in range(fsdp)
                for r in range(replica)
            ],
            axis=1,
        )
        values = hidden[inside].astype(jnp.float32).reshape(tokens * top, width)
        scaled = route_column(turned[1, at]) * back
        hidden_grad[inside] = scaled.reshape(tokens, top, width).astype(jnp.bfloat16)
        column = jnp.sum(values * back, axis=1, keepdims=True)
        gate_turned[at] = route_square(column, tokens, top)

    @pl.when(pl.program_id(0) == pl.num_programs(0) - 1)
    def _():
        gate_grad[...] = gate_turned[...].T


def scale_kernel(place, values, exponents, out, scales):
    _, unit, model_width = values.shape
    blocks = exponents.shape[1]
    width = model_width // blocks
    scales[...] = jnp.exp2(exponents[0].astype(jnp.float32)).T
    rows = scales[pl.ds(pl.multiple_of(place[2] * unit, unit), unit), :]
    for b in range(blocks):
        at = slice(b * width, (b + 1) * width)
        out[0, :, at] = (values[0, :, at].astype(jnp.float32) * rows[:, b : b + 1]).astype(
            jnp.bfloat16
        )


def back_kernel(parts, place, dy, *refs):
    fsdp = parts[0]
    weights, out, rows = refs[:fsdp], refs[-2], refs[-1]
    here, unit, _ = weights[0].shape

    @pl.when(pl.program_id(0) == 0)
    def _():
        for e in range(here):
            for o in range(fsdp):
                at = (e * fsdp + lax.rem(place[1] + o, fsdp)) * unit
                rows[pl.ds(pl.multiple_of(at, unit), unit), :] = weights[o][e]

    back = lax.dot_general(
        dy[...], rows[...], (((1,), (1,)), ((), ())), preferred_element_type=jnp.float32
    )
    out[...] = back.astype(jnp.bfloat16).reshape(out.shape)


def gradient_kernel(parts, place, *refs):
    fsdp, replica = parts
    hids, dys, outs, turned = (
        refs[:replica],
        refs[replica : 2 * replica],
        refs[2 * replica : -1],
        refs[-1],
    )
    here, unit, _ = outs[0].shape

    @pl.when(pl.program_id(0) == 0)
    def _():
        for c in range(replica):
            turned[c] = hids[c][...].reshape(turned.shape[2], turned.shape[1]).T

    total = sum(
        jnp.dot(turned[c], dys[c][...], preferred_element_type=jnp.float32)
        for c in range(replica)
    )
    for e in range(here):
        for o in range(fsdp):
            at = (e * fsdp + o) * unit
            outs[o][e] = total[at : at + unit].astype(outs[o].dtype)


def dense_body(
    out_grad, hidden_saved, gate_probs, expert_ids, weight_q, weight_exp, master, moment1, moment2
):
    tokens, top = expert_ids.shape
    here, rows_here, model_width = weight_q.shape
    width = hidden_saved.shape[2]
    halves, line, pair = lax.axis_size("half"), lax.axis_size("line"), lax.axis_size("pair")
    groups = halves * line * pair
    fsdp, replica = lax.axis_size("fsdp"), lax.axis_size("replica")
    place_of = {name: lax.axis_index(name) for name in ("half", "line", "pair")}
    mf, mr = lax.axis_index("fsdp"), lax.axis_index("replica")
    unit = width // (fsdp * replica)
    block = min(TOKEN_BLOCK * PARTS, tokens)
    lanes = here * fsdp * unit

    def shift(x, axis, by, across=0):
        size = lax.axis_size(axis)
        if not across:
            return lax.ppermute(x, axis, [(i, (i + by) % size) for i in range(size)])
        pairs = [
            (i * pair + j, (i + by) % size * pair + (j + across) % pair)
            for i in range(size)
            for j in range(pair)
        ]
        return lax.ppermute(x, (axis, "pair"), pairs)

    def source_of(b, i, j):
        place = 0
        for name, by in (("half", b), ("line", i), ("pair", j)):
            size = lax.axis_size(name)
            place = place * size + lax.rem(place_of[name] + (size - by), size)
        return place

    def exchange(x):
        x = x.reshape(replica * groups, tokens, lanes)
        x = lax.all_to_all(x, ("replica", "half", "line", "pair"), split_axis=0, concat_axis=0, tiled=True)
        return x.reshape(replica, groups, tokens, lanes)

    place = jnp.stack([mf, mf, mr]).astype(jnp.int32)
    weight_part = pl.pallas_call(
        scale_kernel,
        out_shape=jax.ShapeDtypeStruct((here, unit, model_width), jnp.bfloat16),
        grid_spec=pltpu.PrefetchScalarGridSpec(
            num_scalar_prefetch=1,
            grid=(here,),
            in_specs=[
                pl.BlockSpec((1, unit, model_width), lambda e, p: (e, p[2], 0)),
                pl.BlockSpec((1, weight_exp.shape[2], rows_here), lambda e, p: (e, 0, 0)),
            ],
            out_specs=pl.BlockSpec((1, unit, model_width), lambda e, p: (e, 0, 0)),
            scratch_shapes=[pltpu.VMEM((rows_here, weight_exp.shape[2]), jnp.float32)],
        ),
        compiler_params=pltpu.CompilerParams(vmem_limit_bytes=20 * 2**20),
        name="scale",
    )(place, weight_q, weight_exp.swapaxes(1, 2))

    token_specs = [
        pl.BlockSpec((top, tokens), lambda i, p: (0, 0)),
        pl.BlockSpec((top, tokens), lambda i, p: (0, 0)),
        pl.BlockSpec((block, top, width), lambda i, p: (i, 0, 0)),
    ]
    turned = pltpu.VMEM((2, tokens, top), jnp.float32)
    row_spec = pl.BlockSpec((replica, groups, block, lanes), lambda i, p: (0, 0, i, 0))
    spread = pl.pallas_call(
        lambda *refs: spread_kernel(here, (fsdp, replica), *refs),
        out_shape=jax.ShapeDtypeStruct((replica, groups, tokens, lanes), jnp.bfloat16),
        grid_spec=pltpu.PrefetchScalarGridSpec(
            num_scalar_prefetch=1,
            grid=(tokens // block,),
            in_specs=token_specs,
            out_specs=row_spec,
            scratch_shapes=[turned],
        ),
        compiler_params=pltpu.CompilerParams(vmem_limit_bytes=20 * 2**20),
        name="spread",
    )(place, expert_ids.T, gate_probs.T, hidden_saved)

    dy = {(0, 0, 0): out_grad}
    for b in range(1, halves):
        dy[b, 0, 0] = shift(out_grad, "half", b)
    for i in range(1, line):
        dy[0, i, 0] = shift(out_grad, "line", i)
    for j in range(1, pair):
        dy[0, 0, j] = shift(out_grad, "pair", j)
    dy, spread = lax.optimization_barrier((dy, spread))
    hid = exchange(spread)
    for b in range(1, halves):
        for i in range(1, line):
            dy[b, i, 0] = shift(dy[b, 0, 0], "line", i)
    weight_parts = [weight_part] + [
        lax.ppermute(weight_part, "fsdp", [(f, (f - o) % fsdp) for f in range(fsdp)])
        for o in range(1, fsdp)
    ]
    own = jnp.zeros((groups, tokens, model_width), jnp.bfloat16)
    for b in range(halves):
        for i in range(line):
            for j in range(pair):
                if (b, i, j) not in dy:
                    dy[b, i, j] = (shift(dy[b, 0, 0], "line", i, j) if i else shift(dy[b, 0, 0], "pair", j)) if b else shift(dy[0, i, 0], "pair", j)
                own = lax.dynamic_update_index_in_dim(own, dy[b, i, j], source_of(b, i, j), 0)
    own, weight_parts = lax.optimization_barrier(
        (own.reshape(groups * tokens, model_width), weight_parts)
    )
    dy = [own] + [
        lax.ppermute(own, "replica", [(r, (r - c) % replica) for r in range(replica)])
        for c in range(1, replica)
    ]

    together = max(g for g in (1, 2, 4) if groups % g == 0)
    part_spec = pl.BlockSpec((here, unit, model_width), lambda i, p: (0, 0, 0))
    back = []
    for c in range(replica):
        back = [
            pl.pallas_call(
                lambda *refs: back_kernel((fsdp, replica), *refs),
                out_shape=jax.ShapeDtypeStruct((replica, groups, tokens, lanes), jnp.bfloat16),
                grid_spec=pltpu.PrefetchScalarGridSpec(
                    num_scalar_prefetch=1,
                    grid=(groups // together,),
                    in_specs=[
                        pl.BlockSpec((together * tokens, model_width), lambda i, p: (i, 0))
                    ]
                    + [part_spec] * fsdp
                    + [pl.BlockSpec(memory_space=pl.ANY)] * len(back),
                    out_specs=pl.BlockSpec(
                        (1, together, tokens, lanes),
                        lambda i, p, c=c: (lax.rem(p[2] + c, replica), i, 0, 0),
                    ),
                    scratch_shapes=[pltpu.VMEM((lanes, model_width), jnp.bfloat16)],
                ),
                compiler_params=pltpu.CompilerParams(vmem_limit_bytes=36 * 2**20),
                cost_estimate=pl.CostEstimate(
                    flops=2 * groups * tokens * lanes * model_width,
                    bytes_accessed=2 * groups * tokens * (lanes + model_width),
                    transcendentals=0,
                ),
                input_output_aliases={2 + fsdp: 0} if back else {},
                name="back",
            )(place, dy[c], *weight_parts, *back)
        ]
    back, hid = lax.optimization_barrier((back[0], hid))
    returned = exchange(back)

    columns = min(512, model_width)
    grad_spec = pl.BlockSpec((here, unit, columns), lambda i, p: (0, 0, i))
    grads = pl.pallas_call(
        lambda *refs: gradient_kernel((fsdp, replica), *refs),
        out_shape=[
            jax.ShapeDtypeStruct((here, unit, model_width), jnp.bfloat16 if o else jnp.float32)
            for o in range(fsdp)
        ],
        grid_spec=pltpu.PrefetchScalarGridSpec(
            num_scalar_prefetch=1,
            grid=(model_width // columns,),
            in_specs=[
                pl.BlockSpec(
                    (1, groups, tokens, lanes),
                    lambda i, p, c=c: (lax.rem(p[2] + c, replica), 0, 0, 0),
                )
                for c in range(replica)
            ]
            + [pl.BlockSpec((groups * tokens, columns), lambda i, p: (0, i))] * replica,
            out_specs=[grad_spec] * fsdp,
            scratch_shapes=[pltpu.VMEM((replica, lanes, groups * tokens), jnp.bfloat16)],
        ),
        compiler_params=pltpu.CompilerParams(vmem_limit_bytes=20 * 2**20),
        cost_estimate=pl.CostEstimate(
            flops=2 * replica * groups * tokens * lanes * model_width,
            bytes_accessed=2 * replica * groups * tokens * (lanes + model_width),
            transcendentals=0,
        ),
        name="gradient",
    )(place, *[hid] * replica, *dy)
    gradient = grads[0]
    for o in range(1, fsdp):
        gradient = gradient + lax.ppermute(
            grads[o], "fsdp", [(f, (f + o) % fsdp) for f in range(fsdp)]
        ).astype(jnp.float32)
    first = 0.9 * moment1.astype(jnp.float32) + 0.1 * gradient
    second = 0.95 * moment2.astype(jnp.float32) + 0.05 * gradient * gradient
    update = first / (1.0 - 0.9**20) / (jnp.sqrt(second / (1.0 - 0.95**20)) + 1e-08) + 0.1 * master
    master_new = master - 0.001 * update

    new = (master_new, first.astype(jnp.bfloat16), second.astype(jnp.bfloat16))
    returned, new = lax.optimization_barrier((returned, new))
    hidden_grad, gate_grad = pl.pallas_call(
        lambda *refs: collect_kernel(here, (fsdp, replica), *refs),
        out_shape=[
            jax.ShapeDtypeStruct(hidden_saved.shape, jnp.bfloat16),
            jax.ShapeDtypeStruct((top, tokens), jnp.float32),
        ],
        grid=(tokens // block,),
        in_specs=[
            pl.BlockSpec((top, tokens), lambda i: (0, 0)),
            pl.BlockSpec((top, tokens), lambda i: (0, 0)),
            pl.BlockSpec((block, top, width), lambda i: (i, 0, 0)),
            pl.BlockSpec((replica, groups, block, lanes), lambda i: (0, 0, i, 0)),
        ],
        out_specs=[
            pl.BlockSpec((block, top, width), lambda i: (i, 0, 0)),
            pl.BlockSpec((top, tokens), lambda i: (0, 0)),
        ],
        scratch_shapes=[turned, pltpu.VMEM((tokens, top), jnp.float32)],
        compiler_params=pltpu.CompilerParams(vmem_limit_bytes=20 * 2**20),
        name="collect",
    )(
        expert_ids.T,
        gate_probs.T,
        pltpu.with_memory_space_constraint(hidden_saved, pltpu.HBM),
        returned,
    )
    return (hidden_grad, gate_grad.T) + new


def solution(mesh):
    sizes = dict(mesh.shape)
    devices = mesh.devices.size
    groups = sizes["expert"]

    def mapped(function, mesh, expert):
        rows = P(expert + ("fsdp", "replica"))
        state = P(expert, ("fsdp", "replica"))
        weights = P(expert, "fsdp")
        in_specs = (rows,) * 4 + (weights,) * 2 + (state,) * 3
        out_specs = (rows,) * 2 + (state,) * 3
        return jax.shard_map(
            function, mesh=mesh, in_specs=in_specs, out_specs=out_specs, check_vma=False
        )

    def program(*args):
        tokens, top = args[3].shape[0] // devices, args[3].shape[1]
        dense = min(tokens, 2 * tokens * top // args[4].shape[0]) == tokens
        if not dense or groups % 4 or mesh.axis_names[0] != "expert":
            return mapped(slots_body, mesh, ("expert",))(*args)
        halves = jax.sharding.Mesh(
            mesh.devices.reshape((2, groups // 4, 2) + mesh.devices.shape[1:]),
            ("half", "line", "pair") + mesh.axis_names[1:],
        )
        return mapped(dense_body, halves, ("half", "line", "pair"))(*args)

    return program
```

```python
import jax
import jax.numpy as jnp
from jax import lax
from jax.experimental import pallas as pl
from jax.experimental.pallas import tpu as pltpu
from jax.sharding import PartitionSpec as P

def slots_body(
    out_grad, hidden_saved, gate_probs, expert_ids, weight_q, weight_exp, master, moment1, moment2
):
    tokens_here, top_count = expert_ids.shape
    experts_here, rows_here, model_width = weight_q.shape
    hidden_width = hidden_saved.shape[2]
    expert_groups = lax.axis_size("expert")
    experts_all = expert_groups * experts_here
    capacity = min(tokens_here, 2 * tokens_here * top_count // experts_all)
    routes = tokens_here * top_count
    flat_ids = expert_ids.reshape(-1)
    onehot = (flat_ids[:, None] == jnp.arange(experts_all, dtype=jnp.int32)[None, :]).astype(
        jnp.int32
    )
    rank_in_expert = jnp.sum(jnp.cumsum(onehot, axis=0) * onehot, axis=1) - 1
    slot_index = flat_ids * capacity + rank_in_expert
    route_of_slot = (
        jnp.full((experts_all * capacity,), routes, jnp.int32)
        .at[slot_index]
        .set(jnp.arange(routes, dtype=jnp.int32))
    )
    filled = route_of_slot < routes
    clamped = jnp.minimum(route_of_slot, routes - 1)
    weighted = (
        (gate_probs[..., None] * hidden_saved.astype(jnp.float32))
        .astype(jnp.bfloat16)
        .reshape(routes, hidden_width)
    )
    zero_value = jnp.zeros((), jnp.bfloat16)
    dy_send = jnp.where(filled[:, None], out_grad[clamped // top_count], zero_value)
    weighted_send = jnp.where(filled[:, None], weighted[clamped], zero_value)
    dy_send = dy_send.reshape(expert_groups, experts_here, capacity, model_width)
    weighted_send = weighted_send.reshape(expert_groups, experts_here, capacity, hidden_width)
    recv_dy, recv_weighted = (
        lax.all_to_all(dy_send, "expert", split_axis=0, concat_axis=0, tiled=True),
        lax.all_to_all(weighted_send, "expert", split_axis=0, concat_axis=0, tiled=True),
    )
    scales = jnp.exp2(weight_exp.astype(jnp.float32))
    blocks = weight_exp.shape[2]
    weight_local = (
        (
            weight_q.astype(jnp.float32).reshape(
                experts_here, rows_here, blocks, model_width // blocks
            )
            * scales[..., None]
        )
        .reshape(experts_here, rows_here, model_width)
        .astype(jnp.bfloat16)
    )
    back_rows = jnp.einsum(
        "secd,efd->secf",
        recv_dy,
        lax.all_gather(weight_local, "fsdp", axis=1, tiled=True),
        preferred_element_type=jnp.float32,
    ).astype(jnp.bfloat16)
    returned = lax.all_to_all(back_rows, "expert", split_axis=0, concat_axis=0, tiled=True)
    back_route = returned.reshape(experts_all * capacity, hidden_width)[slot_index].reshape(
        tokens_here, top_count, hidden_width
    )
    back_float = back_route.astype(jnp.float32)
    hidden_grad = (gate_probs[..., None] * back_float).astype(jnp.bfloat16)
    gate_grad = jnp.sum(hidden_saved.astype(jnp.float32) * back_float, axis=-1)
    partial_grad = jnp.einsum(
        "secf,secd->efd", recv_weighted, recv_dy, preferred_element_type=jnp.float32
    )
    gradient = lax.psum_scatter(partial_grad, ("fsdp", "replica"), scatter_dimension=1, tiled=True)
    first = 0.9 * moment1.astype(jnp.float32) + 0.1 * gradient
    second = 0.95 * moment2.astype(jnp.float32) + 0.05 * gradient * gradient
    update = first / (1.0 - 0.9**20) / (jnp.sqrt(second / (1.0 - 0.95**20)) + 1e-08) + 0.1 * master
    master_new = master - 0.001 * update
    return (
        hidden_grad,
        gate_grad,
        master_new,
        first.astype(jnp.bfloat16),
        second.astype(jnp.bfloat16),
    )


VMEM = 100 * 2**20 // 2
TOKEN_BLOCK = 16
PARTS = 4


def pick(index, options):
    result = options[0]
    for number, option in enumerate(options[1:], 1):
        result = jnp.where(index == number, option, result)
    return result


def diagonal(shape):
    return lax.broadcasted_iota(jnp.int32, shape, 1) == lax.broadcasted_iota(jnp.int32, shape, 2)


def route_column(values):
    tokens, top = values.shape
    shape = (tokens, top, top)
    spread = jnp.where(diagonal(shape), jnp.broadcast_to(values[:, None, :], shape), 0.0)
    return jnp.sum(spread.reshape(tokens * top, top), axis=1, keepdims=True)


def route_square(column, tokens, top):
    shape = (tokens, top, top)
    spread = jnp.broadcast_to(column, (tokens * top, top)).reshape(shape)
    return jnp.sum(jnp.where(diagonal(shape), spread, 0.0), axis=1)


def route_match(ids, experts):
    tokens, top = ids.shape
    token = lax.broadcasted_iota(jnp.int32, (tokens, top), 0).astype(jnp.float32)
    keys = route_column(ids * tokens + token).astype(jnp.int32)
    columns = lax.broadcasted_iota(jnp.int32, (tokens * top, experts * tokens), 1)
    return jnp.where(keys == columns, 1.0, 0.0).astype(jnp.bfloat16)


def turn_routes(ids, gate, turned):
    @pl.when(pl.program_id(0) == 0)
    def _():
        turned[0] = ids[...].astype(jnp.float32).T
        turned[1] = gate[...].T


def rows_of_part(step, part, tokens):
    start = pl.program_id(0) * step + part * tokens
    return pl.ds(pl.multiple_of(start, tokens), tokens)


def spread_kernel(here, parts, place, ids, gate, hidden, out, turned):
    fsdp, replica = parts
    step, top, width = hidden.shape
    tokens = min(TOKEN_BLOCK, step)
    groups = out.shape[1]
    unit = width // (fsdp * replica)
    turn_routes(ids, gate, turned)
    for part in range(step // tokens):
        inside = slice(part * tokens, (part + 1) * tokens)
        at = rows_of_part(step, part, tokens)
        match = route_match(turned[0, at], groups * here)
        values = hidden[inside].astype(jnp.float32).reshape(tokens * top, width)
        weighted = (route_column(turned[1, at]) * values).astype(jnp.bfloat16)
        for r in range(replica):
            blocks = [
                weighted[:, (f * replica + r) * unit : (f * replica + r + 1) * unit]
                for f in range(fsdp)
            ]
            share = pick(
                place[1],
                [jnp.concatenate(blocks[f:] + blocks[:f], axis=1) for f in range(fsdp)],
            )
            rows = lax.dot_general(
                match, share, (((0,), (0,)), ((), ())), preferred_element_type=jnp.float32
            ).astype(jnp.bfloat16)
            for g in range(groups):
                for e in range(here):
                    row = (g * here + e) * tokens
                    out[r, g, inside, e * fsdp * unit : (e + 1) * fsdp * unit] = rows[
                        row : row + tokens
                    ]


def collect_kernel(
    here, parts, ids, gate, hidden, backs, hidden_grad, gate_grad, turned, gate_turned
):
    fsdp, replica = parts
    step, top, width = hidden.shape
    tokens = min(TOKEN_BLOCK, step)
    groups = backs.shape[1]
    unit = width // (fsdp * replica)
    turn_routes(ids, gate, turned)
    for part in range(step // tokens):
        inside = slice(part * tokens, (part + 1) * tokens)
        at = rows_of_part(step, part, tokens)
        match = route_match(turned[0, at], groups * here)
        shares = []
        for r in range(replica):
            rows = jnp.concatenate(
                [
                    backs[r, g, inside, e * fsdp * unit : (e + 1) * fsdp * unit]
                    for g in range(groups)
                    for e in range(here)
                ],
                axis=0,
            )
            shares.append(jnp.dot(match, rows, preferred_element_type=jnp.float32))
        back = jnp.concatenate(
            [
                shares[r][:, f * unit : (f + 1) * unit]
                for f in range(fsdp)
                for r in range(replica)
            ],
            axis=1,
        )
        values = hidden[inside].astype(jnp.float32).reshape(tokens * top, width)
        scaled = route_column(turned[1, at]) * back
        hidden_grad[inside] = scaled.reshape(tokens, top, width).astype(jnp.bfloat16)
        column = jnp.sum(values * back, axis=1, keepdims=True)
        gate_turned[at] = route_square(column, tokens, top)

    @pl.when(pl.program_id(0) == pl.num_programs(0) - 1)
    def _():
        gate_grad[...] = gate_turned[...].T


def scale_kernel(place, values, exponents, out, scales):
    _, unit, model_width = values.shape
    blocks = exponents.shape[1]
    width = model_width // blocks
    scales[...] = jnp.exp2(exponents[0].astype(jnp.float32)).T
    rows = scales[pl.ds(pl.multiple_of(place[2] * unit, unit), unit), :]
    for b in range(blocks):
        at = slice(b * width, (b + 1) * width)
        out[0, :, at] = (values[0, :, at].astype(jnp.float32) * rows[:, b : b + 1]).astype(
            jnp.bfloat16
        )


def back_kernel(parts, place, dy, *refs):
    fsdp = parts[0]
    weights, out, rows = refs[:fsdp], refs[-2], refs[-1]
    here, unit, _ = weights[0].shape

    @pl.when(pl.program_id(0) == 0)
    def _():
        for e in range(here):
            for o in range(fsdp):
                at = (e * fsdp + lax.rem(place[1] + o, fsdp)) * unit
                rows[pl.ds(pl.multiple_of(at, unit), unit), :] = weights[o][e]

    back = lax.dot_general(
        dy[...], rows[...], (((1,), (1,)), ((), ())), preferred_element_type=jnp.float32
    )
    out[...] = back.astype(jnp.bfloat16).reshape(out.shape)


def gradient_kernel(parts, place, *refs):
    fsdp, replica = parts
    hids, dys, outs, turned = (
        refs[:replica],
        refs[replica : 2 * replica],
        refs[2 * replica : -1],
        refs[-1],
    )
    here, unit, _ = outs[0].shape

    @pl.when(pl.program_id(0) == 0)
    def _():
        for c in range(replica):
            turned[c] = hids[c][...].reshape(turned.shape[2], turned.shape[1]).T

    total = sum(
        jnp.dot(turned[c], dys[c][...], preferred_element_type=jnp.float32)
        for c in range(replica)
    )
    for e in range(here):
        for o in range(fsdp):
            at = (e * fsdp + o) * unit
            outs[o][e] = total[at : at + unit].astype(outs[o].dtype)


def dense_body(
    out_grad, hidden_saved, gate_probs, expert_ids, weight_q, weight_exp, master, moment1, moment2
):
    tokens, top = expert_ids.shape
    here, rows_here, model_width = weight_q.shape
    width = hidden_saved.shape[2]
    halves, line, pair = lax.axis_size("half"), lax.axis_size("line"), lax.axis_size("pair")
    groups = halves * line * pair
    fsdp, replica = lax.axis_size("fsdp"), lax.axis_size("replica")
    place_of = {name: lax.axis_index(name) for name in ("half", "line", "pair")}
    mf, mr = lax.axis_index("fsdp"), lax.axis_index("replica")
    unit = width // (fsdp * replica)
    block = min(TOKEN_BLOCK * PARTS, tokens)
    lanes = here * fsdp * unit

    def shift(x, axis, by, across=0):
        size = lax.axis_size(axis)
        if not across:
            return lax.ppermute(x, axis, [(i, (i + by) % size) for i in range(size)])
        pairs = [
            (i * pair + j, (i + by) % size * pair + (j + across) % pair)
            for i in range(size)
            for j in range(pair)
        ]
        return lax.ppermute(x, (axis, "pair"), pairs)

    def source_of(b, i, j):
        place = 0
        for name, by in (("half", b), ("line", i), ("pair", j)):
            size = lax.axis_size(name)
            place = place * size + lax.rem(place_of[name] + (size - by), size)
        return place

    def exchange(x):
        x = x.reshape(replica * groups, tokens, lanes)
        x = lax.all_to_all(x, ("replica", "half", "line", "pair"), split_axis=0, concat_axis=0, tiled=True)
        return x.reshape(replica, groups, tokens, lanes)

    place = jnp.stack([mf, mf, mr]).astype(jnp.int32)
    weight_part = pl.pallas_call(
        scale_kernel,
        out_shape=jax.ShapeDtypeStruct((here, unit, model_width), jnp.bfloat16),
        grid_spec=pltpu.PrefetchScalarGridSpec(
            num_scalar_prefetch=1,
            grid=(here,),
            in_specs=[
                pl.BlockSpec((1, unit, model_width), lambda e, p: (e, p[2], 0)),
                pl.BlockSpec((1, weight_exp.shape[2], rows_here), lambda e, p: (e, 0, 0)),
            ],
            out_specs=pl.BlockSpec((1, unit, model_width), lambda e, p: (e, 0, 0)),
            scratch_shapes=[pltpu.VMEM((rows_here, weight_exp.shape[2]), jnp.float32)],
        ),
        compiler_params=pltpu.CompilerParams(vmem_limit_bytes=20 * 2**20),
        name="scale",
    )(place, weight_q, weight_exp.swapaxes(1, 2))

    token_specs = [
        pl.BlockSpec((top, tokens), lambda i, p: (0, 0)),
        pl.BlockSpec((top, tokens), lambda i, p: (0, 0)),
        pl.BlockSpec((block, top, width), lambda i, p: (i, 0, 0)),
    ]
    turned = pltpu.VMEM((2, tokens, top), jnp.float32)
    row_spec = pl.BlockSpec((replica, groups, block, lanes), lambda i, p: (0, 0, i, 0))
    spread = pl.pallas_call(
        lambda *refs: spread_kernel(here, (fsdp, replica), *refs),
        out_shape=jax.ShapeDtypeStruct((replica, groups, tokens, lanes), jnp.bfloat16),
        grid_spec=pltpu.PrefetchScalarGridSpec(
            num_scalar_prefetch=1,
            grid=(tokens // block,),
            in_specs=token_specs,
            out_specs=row_spec,
            scratch_shapes=[turned],
        ),
        compiler_params=pltpu.CompilerParams(vmem_limit_bytes=20 * 2**20),
        name="spread",
    )(place, expert_ids.T, gate_probs.T, hidden_saved)

    dy = {(0, 0, 0): out_grad}
    for b in range(1, halves):
        dy[b, 0, 0] = shift(out_grad, "half", b)
    after, weight_part = lax.optimization_barrier((out_grad, weight_part))
    for i in range(1, line):
        dy[0, i, 0] = shift(after, "line", i)
    for j in range(1, pair):
        dy[0, 0, j] = shift(after, "pair", j)
    keys = [key for key in sorted(dy, reverse=True) if not key[1]]
    held = lax.optimization_barrier([spread] + [dy[key] for key in keys])
    spread = held[0]
    dy.update(zip(keys, held[1:]))
    hid = exchange(spread)
    for b in range(1, halves):
        for i in range(1, line):
            dy[b, i, 0] = shift(dy[b, 0, 0], "line", i)
    weight_parts = [weight_part] + [
        lax.ppermute(weight_part, "fsdp", [(f, (f - o) % fsdp) for f in range(fsdp)])
        for o in range(1, fsdp)
    ]
    own = jnp.zeros((groups, tokens, model_width), jnp.bfloat16)
    for b in range(halves):
        for i in range(line):
            for j in range(pair):
                if (b, i, j) not in dy:
                    dy[b, i, j] = (shift(dy[b, 0, 0], "line", i, j) if i else shift(dy[b, 0, 0], "pair", j)) if b else shift(dy[0, i, 0], "pair", j)
                own = lax.dynamic_update_index_in_dim(own, dy[b, i, j], source_of(b, i, j), 0)
    own, weight_parts = lax.optimization_barrier(
        (own.reshape(groups * tokens, model_width), weight_parts)
    )
    dy = [own] + [
        lax.ppermute(own, "replica", [(r, (r - c) % replica) for r in range(replica)])
        for c in range(1, replica)
    ]

    together = max(g for g in (1, 2, 4) if groups % g == 0)
    part_spec = pl.BlockSpec((here, unit, model_width), lambda i, p: (0, 0, 0))
    back = []
    for c in range(replica):
        back = [
            pl.pallas_call(
                lambda *refs: back_kernel((fsdp, replica), *refs),
                out_shape=jax.ShapeDtypeStruct((replica, groups, tokens, lanes), jnp.bfloat16),
                grid_spec=pltpu.PrefetchScalarGridSpec(
                    num_scalar_prefetch=1,
                    grid=(groups // together,),
                    in_specs=[
                        pl.BlockSpec((together * tokens, model_width), lambda i, p: (i, 0))
                    ]
                    + [part_spec] * fsdp
                    + [pl.BlockSpec(memory_space=pl.ANY)] * len(back),
                    out_specs=pl.BlockSpec(
                        (1, together, tokens, lanes),
                        lambda i, p, c=c: (lax.rem(p[2] + c, replica), i, 0, 0),
                    ),
                    scratch_shapes=[pltpu.VMEM((lanes, model_width), jnp.bfloat16)],
                ),
                compiler_params=pltpu.CompilerParams(vmem_limit_bytes=36 * 2**20),
                cost_estimate=pl.CostEstimate(
                    flops=2 * groups * tokens * lanes * model_width,
                    bytes_accessed=2 * groups * tokens * (lanes + model_width),
                    transcendentals=0,
                ),
                input_output_aliases={2 + fsdp: 0} if back else {},
                name="back",
            )(place, dy[c], *weight_parts, *back)
        ]
    back, hid = lax.optimization_barrier((back[0], hid))
    returned = exchange(back)

    columns = min(512, model_width)
    grad_spec = pl.BlockSpec((here, unit, columns), lambda i, p: (0, 0, i))
    grads = pl.pallas_call(
        lambda *refs: gradient_kernel((fsdp, replica), *refs),
        out_shape=[
            jax.ShapeDtypeStruct((here, unit, model_width), jnp.bfloat16 if o else jnp.float32)
            for o in range(fsdp)
        ],
        grid_spec=pltpu.PrefetchScalarGridSpec(
            num_scalar_prefetch=1,
            grid=(model_width // columns,),
            in_specs=[
                pl.BlockSpec(
                    (1, groups, tokens, lanes),
                    lambda i, p, c=c: (lax.rem(p[2] + c, replica), 0, 0, 0),
                )
                for c in range(replica)
            ]
            + [pl.BlockSpec((groups * tokens, columns), lambda i, p: (0, i))] * replica,
            out_specs=[grad_spec] * fsdp,
            scratch_shapes=[pltpu.VMEM((replica, lanes, groups * tokens), jnp.bfloat16)],
        ),
        compiler_params=pltpu.CompilerParams(vmem_limit_bytes=20 * 2**20),
        cost_estimate=pl.CostEstimate(
            flops=2 * replica * groups * tokens * lanes * model_width,
            bytes_accessed=2 * replica * groups * tokens * (lanes + model_width),
            transcendentals=0,
        ),
        name="gradient",
    )(place, *[hid] * replica, *dy)
    gradient = grads[0]
    for o in range(1, fsdp):
        gradient = gradient + lax.ppermute(
            grads[o], "fsdp", [(f, (f + o) % fsdp) for f in range(fsdp)]
        ).astype(jnp.float32)
    first = 0.9 * moment1.astype(jnp.float32) + 0.1 * gradient
    second = 0.95 * moment2.astype(jnp.float32) + 0.05 * gradient * gradient
    update = first / (1.0 - 0.9**20) / (jnp.sqrt(second / (1.0 - 0.95**20)) + 1e-08) + 0.1 * master
    master_new = master - 0.001 * update

    new = (master_new, first.astype(jnp.bfloat16), second.astype(jnp.bfloat16))
    returned, new = lax.optimization_barrier((returned, new))
    hidden_grad, gate_grad = pl.pallas_call(
        lambda *refs: collect_kernel(here, (fsdp, replica), *refs),
        out_shape=[
            jax.ShapeDtypeStruct(hidden_saved.shape, jnp.bfloat16),
            jax.ShapeDtypeStruct((top, tokens), jnp.float32),
        ],
        grid=(tokens // block,),
        in_specs=[
            pl.BlockSpec((top, tokens), lambda i: (0, 0)),
            pl.BlockSpec((top, tokens), lambda i: (0, 0)),
            pl.BlockSpec((block, top, width), lambda i: (i, 0, 0)),
            pl.BlockSpec((replica, groups, block, lanes), lambda i: (0, 0, i, 0)),
        ],
        out_specs=[
            pl.BlockSpec((block, top, width), lambda i: (i, 0, 0)),
            pl.BlockSpec((top, tokens), lambda i: (0, 0)),
        ],
        scratch_shapes=[turned, pltpu.VMEM((tokens, top), jnp.float32)],
        compiler_params=pltpu.CompilerParams(vmem_limit_bytes=20 * 2**20),
        name="collect",
    )(
        expert_ids.T,
        gate_probs.T,
        pltpu.with_memory_space_constraint(hidden_saved, pltpu.HBM),
        returned,
    )
    return (hidden_grad, gate_grad.T) + new


def solution(mesh):
    sizes = dict(mesh.shape)
    devices = mesh.devices.size
    groups = sizes["expert"]

    def mapped(function, mesh, expert):
        rows = P(expert + ("fsdp", "replica"))
        state = P(expert, ("fsdp", "replica"))
        weights = P(expert, "fsdp")
        in_specs = (rows,) * 4 + (weights,) * 2 + (state,) * 3
        out_specs = (rows,) * 2 + (state,) * 3
        return jax.shard_map(
            function, mesh=mesh, in_specs=in_specs, out_specs=out_specs, check_vma=False
        )

    def program(*args):
        tokens, top = args[3].shape[0] // devices, args[3].shape[1]
        dense = min(tokens, 2 * tokens * top // args[4].shape[0]) == tokens
        if not dense or groups % 4 or mesh.axis_names[0] != "expert":
            return mapped(slots_body, mesh, ("expert",))(*args)
        halves = jax.sharding.Mesh(
            mesh.devices.reshape((2, groups // 4, 2) + mesh.devices.shape[1:]),
            ("half", "line", "pair") + mesh.axis_names[1:],
        )
        return mapped(dense_body, halves, ("half", "line", "pair"))(*args)

    return program
```

```python
import jax
import jax.numpy as jnp
from jax import lax
from jax.experimental import pallas as pl
from jax.experimental.pallas import tpu as pltpu
from jax.sharding import PartitionSpec as P

def slots_body(
    out_grad, hidden_saved, gate_probs, expert_ids, weight_q, weight_exp, master, moment1, moment2
):
    tokens_here, top_count = expert_ids.shape
    experts_here, rows_here, model_width = weight_q.shape
    hidden_width = hidden_saved.shape[2]
    expert_groups = lax.axis_size("expert")
    experts_all = expert_groups * experts_here
    capacity = min(tokens_here, 2 * tokens_here * top_count // experts_all)
    routes = tokens_here * top_count
    flat_ids = expert_ids.reshape(-1)
    onehot = (flat_ids[:, None] == jnp.arange(experts_all, dtype=jnp.int32)[None, :]).astype(
        jnp.int32
    )
    rank_in_expert = jnp.sum(jnp.cumsum(onehot, axis=0) * onehot, axis=1) - 1
    slot_index = flat_ids * capacity + rank_in_expert
    route_of_slot = (
        jnp.full((experts_all * capacity,), routes, jnp.int32)
        .at[slot_index]
        .set(jnp.arange(routes, dtype=jnp.int32))
    )
    filled = route_of_slot < routes
    clamped = jnp.minimum(route_of_slot, routes - 1)
    weighted = (
        (gate_probs[..., None] * hidden_saved.astype(jnp.float32))
        .astype(jnp.bfloat16)
        .reshape(routes, hidden_width)
    )
    zero_value = jnp.zeros((), jnp.bfloat16)
    dy_send = jnp.where(filled[:, None], out_grad[clamped // top_count], zero_value)
    weighted_send = jnp.where(filled[:, None], weighted[clamped], zero_value)
    dy_send = dy_send.reshape(expert_groups, experts_here, capacity, model_width)
    weighted_send = weighted_send.reshape(expert_groups, experts_here, capacity, hidden_width)
    recv_dy, recv_weighted = (
        lax.all_to_all(dy_send, "expert", split_axis=0, concat_axis=0, tiled=True),
        lax.all_to_all(weighted_send, "expert", split_axis=0, concat_axis=0, tiled=True),
    )
    scales = jnp.exp2(weight_exp.astype(jnp.float32))
    blocks = weight_exp.shape[2]
    weight_local = (
        (
            weight_q.astype(jnp.float32).reshape(
                experts_here, rows_here, blocks, model_width // blocks
            )
            * scales[..., None]
        )
        .reshape(experts_here, rows_here, model_width)
        .astype(jnp.bfloat16)
    )
    back_rows = jnp.einsum(
        "secd,efd->secf",
        recv_dy,
        lax.all_gather(weight_local, "fsdp", axis=1, tiled=True),
        preferred_element_type=jnp.float32,
    ).astype(jnp.bfloat16)
    returned = lax.all_to_all(back_rows, "expert", split_axis=0, concat_axis=0, tiled=True)
    back_route = returned.reshape(experts_all * capacity, hidden_width)[slot_index].reshape(
        tokens_here, top_count, hidden_width
    )
    back_float = back_route.astype(jnp.float32)
    hidden_grad = (gate_probs[..., None] * back_float).astype(jnp.bfloat16)
    gate_grad = jnp.sum(hidden_saved.astype(jnp.float32) * back_float, axis=-1)
    partial_grad = jnp.einsum(
        "secf,secd->efd", recv_weighted, recv_dy, preferred_element_type=jnp.float32
    )
    gradient = lax.psum_scatter(partial_grad, ("fsdp", "replica"), scatter_dimension=1, tiled=True)
    first = 0.9 * moment1.astype(jnp.float32) + 0.1 * gradient
    second = 0.95 * moment2.astype(jnp.float32) + 0.05 * gradient * gradient
    update = first / (1.0 - 0.9**20) / (jnp.sqrt(second / (1.0 - 0.95**20)) + 1e-08) + 0.1 * master
    master_new = master - 0.001 * update
    return (
        hidden_grad,
        gate_grad,
        master_new,
        first.astype(jnp.bfloat16),
        second.astype(jnp.bfloat16),
    )


VMEM = 100 * 2**20 // 2
TOKEN_BLOCK = 16
PARTS = 4


def pick(index, options):
    result = options[0]
    for number, option in enumerate(options[1:], 1):
        result = jnp.where(index == number, option, result)
    return result


def diagonal(shape):
    return lax.broadcasted_iota(jnp.int32, shape, 1) == lax.broadcasted_iota(jnp.int32, shape, 2)


def route_column(values):
    tokens, top = values.shape
    shape = (tokens, top, top)
    spread = jnp.where(diagonal(shape), jnp.broadcast_to(values[:, None, :], shape), 0.0)
    return jnp.sum(spread.reshape(tokens * top, top), axis=1, keepdims=True)


def route_square(column, tokens, top):
    shape = (tokens, top, top)
    spread = jnp.broadcast_to(column, (tokens * top, top)).reshape(shape)
    return jnp.sum(jnp.where(diagonal(shape), spread, 0.0), axis=1)


def route_match(ids, experts):
    tokens, top = ids.shape
    token = lax.broadcasted_iota(jnp.int32, (tokens, top), 0).astype(jnp.float32)
    keys = route_column(ids * tokens + token).astype(jnp.int32)
    columns = lax.broadcasted_iota(jnp.int32, (tokens * top, experts * tokens), 1)
    return jnp.where(keys == columns, 1.0, 0.0).astype(jnp.bfloat16)


def turn_routes(ids, gate, turned):
    @pl.when(pl.program_id(0) == 0)
    def _():
        turned[0] = ids[...].astype(jnp.float32).T
        turned[1] = gate[...].T


def rows_of_part(step, part, tokens):
    start = pl.program_id(0) * step + part * tokens
    return pl.ds(pl.multiple_of(start, tokens), tokens)


def spread_kernel(here, parts, place, ids, gate, hidden, out, turned):
    fsdp, replica = parts
    step, top, width = hidden.shape
    tokens = min(TOKEN_BLOCK, step)
    groups = out.shape[1]
    unit = width // (fsdp * replica)
    turn_routes(ids, gate, turned)
    for part in range(step // tokens):
        inside = slice(part * tokens, (part + 1) * tokens)
        at = rows_of_part(step, part, tokens)
        match = route_match(turned[0, at], groups * here)
        values = hidden[inside].astype(jnp.float32).reshape(tokens * top, width)
        weighted = (route_column(turned[1, at]) * values).astype(jnp.bfloat16)
        for r in range(replica):
            blocks = [
                weighted[:, (f * replica + r) * unit : (f * replica + r + 1) * unit]
                for f in range(fsdp)
            ]
            share = pick(
                place[1],
                [jnp.concatenate(blocks[f:] + blocks[:f], axis=1) for f in range(fsdp)],
            )
            rows = lax.dot_general(
                match, share, (((0,), (0,)), ((), ())), preferred_element_type=jnp.float32
            ).astype(jnp.bfloat16)
            for g in range(groups):
                for e in range(here):
                    row = (g * here + e) * tokens
                    out[r, g, inside, e * fsdp * unit : (e + 1) * fsdp * unit] = rows[
                        row : row + tokens
                    ]


def collect_kernel(
    here, parts, ids, gate, hidden, backs, hidden_grad, gate_grad, turned, gate_turned
):
    fsdp, replica = parts
    step, top, width = hidden.shape
    tokens = min(TOKEN_BLOCK, step)
    groups = backs.shape[1]
    unit = width // (fsdp * replica)
    turn_routes(ids, gate, turned)
    for part in range(step // tokens):
        inside = slice(part * tokens, (part + 1) * tokens)
        at = rows_of_part(step, part, tokens)
        match = route_match(turned[0, at], groups * here)
        rows = jnp.concatenate(
            [
                jnp.concatenate(
                    [
                        backs[r, g, inside, e * fsdp * unit : (e + 1) * fsdp * unit]
                        for r in range(replica)
                    ],
                    axis=1,
                )
                for g in range(groups)
                for e in range(here)
            ],
            axis=0,
        )
        found = jnp.dot(match, rows, preferred_element_type=jnp.float32)
        back = jnp.concatenate(
            [
                found[:, (r * fsdp + f) * unit : (r * fsdp + f + 1) * unit]
                for f in range(fsdp)
                for r in range(replica)
            ],
            axis=1,
        )
        values = hidden[inside].astype(jnp.float32).reshape(tokens * top, width)
        scaled = route_column(turned[1, at]) * back
        hidden_grad[inside] = scaled.reshape(tokens, top, width).astype(jnp.bfloat16)
        column = jnp.sum(values * back, axis=1, keepdims=True)
        gate_turned[at] = route_square(column, tokens, top)

    @pl.when(pl.program_id(0) == pl.num_programs(0) - 1)
    def _():
        gate_grad[...] = gate_turned[...].T


def scale_kernel(place, values, exponents, out, scales):
    _, unit, model_width = values.shape
    blocks = exponents.shape[1]
    width = model_width // blocks
    scales[...] = jnp.exp2(exponents[0].astype(jnp.float32)).T
    rows = scales[pl.ds(pl.multiple_of(place[2] * unit, unit), unit), :]
    for b in range(blocks):
        at = slice(b * width, (b + 1) * width)
        out[0, :, at] = (values[0, :, at].astype(jnp.float32) * rows[:, b : b + 1]).astype(
            jnp.bfloat16
        )


def back_kernel(parts, place, dy, *refs):
    fsdp = parts[0]
    weights, out, rows = refs[:fsdp], refs[-2], refs[-1]
    here, unit, _ = weights[0].shape

    @pl.when(pl.program_id(0) == 0)
    def _():
        for e in range(here):
            for o in range(fsdp):
                at = (e * fsdp + lax.rem(place[1] + o, fsdp)) * unit
                rows[pl.ds(pl.multiple_of(at, unit), unit), :] = weights[o][e]

    back = lax.dot_general(
        dy[...], rows[...], (((1,), (1,)), ((), ())), preferred_element_type=jnp.float32
    )
    out[...] = back.astype(jnp.bfloat16).reshape(out.shape)


def gradient_kernel(parts, place, *refs):
    fsdp, replica = parts
    hids, dys, outs, turned = (
        refs[:replica],
        refs[replica : 2 * replica],
        refs[2 * replica : -1],
        refs[-1],
    )
    here, unit, _ = outs[0].shape

    @pl.when(pl.program_id(0) == 0)
    def _():
        for c in range(replica):
            turned[c] = hids[c][...].reshape(turned.shape[2], turned.shape[1]).T

    total = sum(
        jnp.dot(turned[c], dys[c][...], preferred_element_type=jnp.float32)
        for c in range(replica)
    )
    for e in range(here):
        for o in range(fsdp):
            at = (e * fsdp + o) * unit
            outs[o][e] = total[at : at + unit].astype(outs[o].dtype)


def dense_body(
    out_grad, hidden_saved, gate_probs, expert_ids, weight_q, weight_exp, master, moment1, moment2
):
    tokens, top = expert_ids.shape
    here, rows_here, model_width = weight_q.shape
    width = hidden_saved.shape[2]
    halves, line, pair = lax.axis_size("half"), lax.axis_size("line"), lax.axis_size("pair")
    groups = halves * line * pair
    fsdp, replica = lax.axis_size("fsdp"), lax.axis_size("replica")
    place_of = {name: lax.axis_index(name) for name in ("half", "line", "pair")}
    mf, mr = lax.axis_index("fsdp"), lax.axis_index("replica")
    unit = width // (fsdp * replica)
    block = min(TOKEN_BLOCK * PARTS, tokens)
    lanes = here * fsdp * unit

    def shift(x, axis, by, across=0):
        size = lax.axis_size(axis)
        if not across:
            return lax.ppermute(x, axis, [(i, (i + by) % size) for i in range(size)])
        pairs = [
            (i * pair + j, (i + by) % size * pair + (j + across) % pair)
            for i in range(size)
            for j in range(pair)
        ]
        return lax.ppermute(x, (axis, "pair"), pairs)

    def source_of(b, i, j):
        place = 0
        for name, by in (("half", b), ("line", i), ("pair", j)):
            size = lax.axis_size(name)
            place = place * size + lax.rem(place_of[name] + (size - by), size)
        return place

    def exchange(x):
        x = x.reshape(replica * groups, tokens, lanes)
        x = lax.all_to_all(x, ("replica", "half", "line", "pair"), split_axis=0, concat_axis=0, tiled=True)
        return x.reshape(replica, groups, tokens, lanes)

    place = jnp.stack([mf, mf, mr]).astype(jnp.int32)
    weight_part = pl.pallas_call(
        scale_kernel,
        out_shape=jax.ShapeDtypeStruct((here, unit, model_width), jnp.bfloat16),
        grid_spec=pltpu.PrefetchScalarGridSpec(
            num_scalar_prefetch=1,
            grid=(here,),
            in_specs=[
                pl.BlockSpec((1, unit, model_width), lambda e, p: (e, p[2], 0)),
                pl.BlockSpec((1, weight_exp.shape[2], rows_here), lambda e, p: (e, 0, 0)),
            ],
            out_specs=pl.BlockSpec((1, unit, model_width), lambda e, p: (e, 0, 0)),
            scratch_shapes=[pltpu.VMEM((rows_here, weight_exp.shape[2]), jnp.float32)],
        ),
        compiler_params=pltpu.CompilerParams(vmem_limit_bytes=20 * 2**20),
        name="scale",
    )(place, weight_q, weight_exp.swapaxes(1, 2))

    token_specs = [
        pl.BlockSpec((top, tokens), lambda i, p: (0, 0)),
        pl.BlockSpec((top, tokens), lambda i, p: (0, 0)),
        pl.BlockSpec((block, top, width), lambda i, p: (i, 0, 0)),
    ]
    turned = pltpu.VMEM((2, tokens, top), jnp.float32)
    row_spec = pl.BlockSpec((replica, groups, block, lanes), lambda i, p: (0, 0, i, 0))
    spread = pl.pallas_call(
        lambda *refs: spread_kernel(here, (fsdp, replica), *refs),
        out_shape=jax.ShapeDtypeStruct((replica, groups, tokens, lanes), jnp.bfloat16),
        grid_spec=pltpu.PrefetchScalarGridSpec(
            num_scalar_prefetch=1,
            grid=(tokens // block,),
            in_specs=token_specs,
            out_specs=row_spec,
            scratch_shapes=[turned],
        ),
        compiler_params=pltpu.CompilerParams(vmem_limit_bytes=20 * 2**20),
        name="spread",
    )(place, expert_ids.T, gate_probs.T, hidden_saved)

    dy = {(0, 0, 0): out_grad}
    for b in range(1, halves):
        dy[b, 0, 0] = shift(out_grad, "half", b)
    after, weight_part = lax.optimization_barrier((out_grad, weight_part))
    for i in range(1, line):
        dy[0, i, 0] = shift(after, "line", i)
    for j in range(1, pair):
        dy[0, 0, j] = shift(after, "pair", j)
    keys = [key for key in sorted(dy, reverse=True) if not key[1]]
    held = lax.optimization_barrier([spread] + [dy[key] for key in keys])
    spread = held[0]
    dy.update(zip(keys, held[1:]))
    hid = exchange(spread)
    for b in range(1, halves):
        for i in range(1, line):
            dy[b, i, 0] = shift(dy[b, 0, 0], "line", i)
    weight_parts = [weight_part] + [
        lax.ppermute(weight_part, "fsdp", [(f, (f - o) % fsdp) for f in range(fsdp)])
        for o in range(1, fsdp)
    ]
    own = jnp.zeros((groups, tokens, model_width), jnp.bfloat16)
    for b in range(halves):
        for i in range(line):
            for j in range(pair):
                if (b, i, j) not in dy:
                    dy[b, i, j] = (shift(dy[b, 0, 0], "line", i, j) if i else shift(dy[b, 0, 0], "pair", j)) if b else shift(dy[0, i, 0], "pair", j)
                own = lax.dynamic_update_index_in_dim(own, dy[b, i, j], source_of(b, i, j), 0)
    own, weight_parts = lax.optimization_barrier(
        (own.reshape(groups * tokens, model_width), weight_parts)
    )
    dy = [own] + [
        lax.ppermute(own, "replica", [(r, (r - c) % replica) for r in range(replica)])
        for c in range(1, replica)
    ]

    together = max(g for g in (1, 2, 4) if groups % g == 0)
    part_spec = pl.BlockSpec((here, unit, model_width), lambda i, p: (0, 0, 0))
    back = []
    for c in range(replica):
        back = [
            pl.pallas_call(
                lambda *refs: back_kernel((fsdp, replica), *refs),
                out_shape=jax.ShapeDtypeStruct((replica, groups, tokens, lanes), jnp.bfloat16),
                grid_spec=pltpu.PrefetchScalarGridSpec(
                    num_scalar_prefetch=1,
                    grid=(groups // together,),
                    in_specs=[
                        pl.BlockSpec((together * tokens, model_width), lambda i, p: (i, 0))
                    ]
                    + [part_spec] * fsdp
                    + [pl.BlockSpec(memory_space=pl.ANY)] * len(back),
                    out_specs=pl.BlockSpec(
                        (1, together, tokens, lanes),
                        lambda i, p, c=c: (lax.rem(p[2] + c, replica), i, 0, 0),
                    ),
                    scratch_shapes=[pltpu.VMEM((lanes, model_width), jnp.bfloat16)],
                ),
                compiler_params=pltpu.CompilerParams(vmem_limit_bytes=36 * 2**20),
                cost_estimate=pl.CostEstimate(
                    flops=2 * groups * tokens * lanes * model_width,
                    bytes_accessed=2 * groups * tokens * (lanes + model_width),
                    transcendentals=0,
                ),
                input_output_aliases={2 + fsdp: 0} if back else {},
                name="back",
            )(place, dy[c], *weight_parts, *back)
        ]
    back, hid = lax.optimization_barrier((back[0], hid))
    returned = exchange(back)

    columns = min(512, model_width)
    grad_spec = pl.BlockSpec((here, unit, columns), lambda i, p: (0, 0, i))
    grads = pl.pallas_call(
        lambda *refs: gradient_kernel((fsdp, replica), *refs),
        out_shape=[
            jax.ShapeDtypeStruct((here, unit, model_width), jnp.bfloat16 if o else jnp.float32)
            for o in range(fsdp)
        ],
        grid_spec=pltpu.PrefetchScalarGridSpec(
            num_scalar_prefetch=1,
            grid=(model_width // columns,),
            in_specs=[
                pl.BlockSpec(
                    (1, groups, tokens, lanes),
                    lambda i, p, c=c: (lax.rem(p[2] + c, replica), 0, 0, 0),
                )
                for c in range(replica)
            ]
            + [pl.BlockSpec((groups * tokens, columns), lambda i, p: (0, i))] * replica,
            out_specs=[grad_spec] * fsdp,
            scratch_shapes=[pltpu.VMEM((replica, lanes, groups * tokens), jnp.bfloat16)],
        ),
        compiler_params=pltpu.CompilerParams(vmem_limit_bytes=20 * 2**20),
        cost_estimate=pl.CostEstimate(
            flops=2 * replica * groups * tokens * lanes * model_width,
            bytes_accessed=2 * replica * groups * tokens * (lanes + model_width),
            transcendentals=0,
        ),
        name="gradient",
    )(place, *[hid] * replica, *dy)
    gradient = grads[0]
    for o in range(1, fsdp):
        gradient = gradient + lax.ppermute(
            grads[o], "fsdp", [(f, (f + o) % fsdp) for f in range(fsdp)]
        ).astype(jnp.float32)
    first = 0.9 * moment1.astype(jnp.float32) + 0.1 * gradient
    second = 0.95 * moment2.astype(jnp.float32) + 0.05 * gradient * gradient
    update = first / (1.0 - 0.9**20) / (jnp.sqrt(second / (1.0 - 0.95**20)) + 1e-08) + 0.1 * master
    master_new = master - 0.001 * update

    new = (master_new, first.astype(jnp.bfloat16), second.astype(jnp.bfloat16))
    returned, new = lax.optimization_barrier((returned, new))
    hidden_grad, gate_grad = pl.pallas_call(
        lambda *refs: collect_kernel(here, (fsdp, replica), *refs),
        out_shape=[
            jax.ShapeDtypeStruct(hidden_saved.shape, jnp.bfloat16),
            jax.ShapeDtypeStruct((top, tokens), jnp.float32),
        ],
        grid=(tokens // block,),
        in_specs=[
            pl.BlockSpec((top, tokens), lambda i: (0, 0)),
            pl.BlockSpec((top, tokens), lambda i: (0, 0)),
            pl.BlockSpec((block, top, width), lambda i: (i, 0, 0)),
            pl.BlockSpec((replica, groups, block, lanes), lambda i: (0, 0, i, 0)),
        ],
        out_specs=[
            pl.BlockSpec((block, top, width), lambda i: (i, 0, 0)),
            pl.BlockSpec((top, tokens), lambda i: (0, 0)),
        ],
        scratch_shapes=[turned, pltpu.VMEM((tokens, top), jnp.float32)],
        compiler_params=pltpu.CompilerParams(vmem_limit_bytes=20 * 2**20),
        name="collect",
    )(
        expert_ids.T,
        gate_probs.T,
        pltpu.with_memory_space_constraint(hidden_saved, pltpu.HBM),
        returned,
    )
    return (hidden_grad, gate_grad.T) + new


def solution(mesh):
    sizes = dict(mesh.shape)
    devices = mesh.devices.size
    groups = sizes["expert"]

    def mapped(function, mesh, expert):
        rows = P(expert + ("fsdp", "replica"))
        state = P(expert, ("fsdp", "replica"))
        weights = P(expert, "fsdp")
        in_specs = (rows,) * 4 + (weights,) * 2 + (state,) * 3
        out_specs = (rows,) * 2 + (state,) * 3
        return jax.shard_map(
            function, mesh=mesh, in_specs=in_specs, out_specs=out_specs, check_vma=False
        )

    def program(*args):
        tokens, top = args[3].shape[0] // devices, args[3].shape[1]
        dense = min(tokens, 2 * tokens * top // args[4].shape[0]) == tokens
        if not dense or groups % 4 or mesh.axis_names[0] != "expert":
            return mapped(slots_body, mesh, ("expert",))(*args)
        halves = jax.sharding.Mesh(
            mesh.devices.reshape((2, groups // 4, 2) + mesh.devices.shape[1:]),
            ("half", "line", "pair") + mesh.axis_names[1:],
        )
        return mapped(dense_body, halves, ("half", "line", "pair"))(*args)

    return program
```

```python
import jax
import jax.numpy as jnp
from jax import lax
from jax.experimental import pallas as pl
from jax.experimental.pallas import tpu as pltpu
from jax.sharding import PartitionSpec as P

def slots_body(
    out_grad, hidden_saved, gate_probs, expert_ids, weight_q, weight_exp, master, moment1, moment2
):
    tokens_here, top_count = expert_ids.shape
    experts_here, rows_here, model_width = weight_q.shape
    hidden_width = hidden_saved.shape[2]
    expert_groups = lax.axis_size("expert")
    experts_all = expert_groups * experts_here
    capacity = min(tokens_here, 2 * tokens_here * top_count // experts_all)
    routes = tokens_here * top_count
    flat_ids = expert_ids.reshape(-1)
    onehot = (flat_ids[:, None] == jnp.arange(experts_all, dtype=jnp.int32)[None, :]).astype(
        jnp.int32
    )
    rank_in_expert = jnp.sum(jnp.cumsum(onehot, axis=0) * onehot, axis=1) - 1
    slot_index = flat_ids * capacity + rank_in_expert
    route_of_slot = (
        jnp.full((experts_all * capacity,), routes, jnp.int32)
        .at[slot_index]
        .set(jnp.arange(routes, dtype=jnp.int32))
    )
    filled = route_of_slot < routes
    clamped = jnp.minimum(route_of_slot, routes - 1)
    weighted = (
        (gate_probs[..., None] * hidden_saved.astype(jnp.float32))
        .astype(jnp.bfloat16)
        .reshape(routes, hidden_width)
    )
    zero_value = jnp.zeros((), jnp.bfloat16)
    dy_send = jnp.where(filled[:, None], out_grad[clamped // top_count], zero_value)
    weighted_send = jnp.where(filled[:, None], weighted[clamped], zero_value)
    dy_send = dy_send.reshape(expert_groups, experts_here, capacity, model_width)
    weighted_send = weighted_send.reshape(expert_groups, experts_here, capacity, hidden_width)
    recv_dy, recv_weighted = (
        lax.all_to_all(dy_send, "expert", split_axis=0, concat_axis=0, tiled=True),
        lax.all_to_all(weighted_send, "expert", split_axis=0, concat_axis=0, tiled=True),
    )
    scales = jnp.exp2(weight_exp.astype(jnp.float32))
    blocks = weight_exp.shape[2]
    weight_local = (
        (
            weight_q.astype(jnp.float32).reshape(
                experts_here, rows_here, blocks, model_width // blocks
            )
            * scales[..., None]
        )
        .reshape(experts_here, rows_here, model_width)
        .astype(jnp.bfloat16)
    )
    back_rows = jnp.einsum(
        "secd,efd->secf",
        recv_dy,
        lax.all_gather(weight_local, "fsdp", axis=1, tiled=True),
        preferred_element_type=jnp.float32,
    ).astype(jnp.bfloat16)
    returned = lax.all_to_all(back_rows, "expert", split_axis=0, concat_axis=0, tiled=True)
    back_route = returned.reshape(experts_all * capacity, hidden_width)[slot_index].reshape(
        tokens_here, top_count, hidden_width
    )
    back_float = back_route.astype(jnp.float32)
    hidden_grad = (gate_probs[..., None] * back_float).astype(jnp.bfloat16)
    gate_grad = jnp.sum(hidden_saved.astype(jnp.float32) * back_float, axis=-1)
    partial_grad = jnp.einsum(
        "secf,secd->efd", recv_weighted, recv_dy, preferred_element_type=jnp.float32
    )
    gradient = lax.psum_scatter(partial_grad, ("fsdp", "replica"), scatter_dimension=1, tiled=True)
    first = 0.9 * moment1.astype(jnp.float32) + 0.1 * gradient
    second = 0.95 * moment2.astype(jnp.float32) + 0.05 * gradient * gradient
    update = first / (1.0 - 0.9**20) / (jnp.sqrt(second / (1.0 - 0.95**20)) + 1e-08) + 0.1 * master
    master_new = master - 0.001 * update
    return (
        hidden_grad,
        gate_grad,
        master_new,
        first.astype(jnp.bfloat16),
        second.astype(jnp.bfloat16),
    )


VMEM = 100 * 2**20 // 2
TOKEN_BLOCK = 16
PARTS = 4


def pick(index, options):
    result = options[0]
    for number, option in enumerate(options[1:], 1):
        result = jnp.where(index == number, option, result)
    return result


def diagonal(shape):
    return lax.broadcasted_iota(jnp.int32, shape, 1) == lax.broadcasted_iota(jnp.int32, shape, 2)


def route_column(values):
    tokens, top = values.shape
    shape = (tokens, top, top)
    spread = jnp.where(diagonal(shape), jnp.broadcast_to(values[:, None, :], shape), 0.0)
    return jnp.sum(spread.reshape(tokens * top, top), axis=1, keepdims=True)


def route_square(column, tokens, top):
    shape = (tokens, top, top)
    spread = jnp.broadcast_to(column, (tokens * top, top)).reshape(shape)
    return jnp.sum(jnp.where(diagonal(shape), spread, 0.0), axis=1)


def route_match(ids, experts):
    tokens, top = ids.shape
    token = lax.broadcasted_iota(jnp.int32, (tokens, top), 0).astype(jnp.float32)
    keys = route_column(ids * tokens + token).astype(jnp.int32)
    columns = lax.broadcasted_iota(jnp.int32, (tokens * top, experts * tokens), 1)
    return jnp.where(keys == columns, 1.0, 0.0).astype(jnp.bfloat16)


def turn_routes(ids, gate, turned):
    @pl.when(pl.program_id(0) == 0)
    def _():
        turned[0] = ids[...].astype(jnp.float32).T
        turned[1] = gate[...].T


def rows_of_part(step, part, tokens):
    start = pl.program_id(0) * step + part * tokens
    return pl.ds(pl.multiple_of(start, tokens), tokens)


def spread_kernel(here, parts, place, ids, gate, hidden, out, turned):
    fsdp, replica = parts
    step, top, width = hidden.shape
    tokens = min(TOKEN_BLOCK, step)
    groups = out.shape[1]
    unit = width // (fsdp * replica)
    turn_routes(ids, gate, turned)
    for part in range(step // tokens):
        inside = slice(part * tokens, (part + 1) * tokens)
        at = rows_of_part(step, part, tokens)
        match = route_match(turned[0, at], groups * here)
        values = hidden[inside].astype(jnp.float32).reshape(tokens * top, width)
        weighted = (route_column(turned[1, at]) * values).astype(jnp.bfloat16)
        for r in range(replica):
            blocks = [
                weighted[:, (f * replica + r) * unit : (f * replica + r + 1) * unit]
                for f in range(fsdp)
            ]
            share = pick(
                place[1],
                [jnp.concatenate(blocks[f:] + blocks[:f], axis=1) for f in range(fsdp)],
            )
            rows = lax.dot_general(
                match, share, (((0,), (0,)), ((), ())), preferred_element_type=jnp.float32
            ).astype(jnp.bfloat16)
            for g in range(groups):
                for e in range(here):
                    row = (g * here + e) * tokens
                    out[r, g, inside, e * fsdp * unit : (e + 1) * fsdp * unit] = rows[
                        row : row + tokens
                    ]


def collect_kernel(
    here, parts, ids, gate, hidden, backs, hidden_grad, gate_grad, turned, gate_turned
):
    fsdp, replica = parts
    step, top, width = hidden.shape
    tokens = min(TOKEN_BLOCK, step)
    groups = backs.shape[1]
    unit = width // (fsdp * replica)
    turn_routes(ids, gate, turned)
    for part in range(step // tokens):
        inside = slice(part * tokens, (part + 1) * tokens)
        at = rows_of_part(step, part, tokens)
        match = route_match(turned[0, at], groups * here)
        rows = jnp.concatenate(
            [
                jnp.concatenate(
                    [
                        backs[r, g, inside, e * fsdp * unit : (e + 1) * fsdp * unit]
                        for r in range(replica)
                    ],
                    axis=1,
                )
                for g in range(groups)
                for e in range(here)
            ],
            axis=0,
        )
        found = jnp.dot(match, rows, preferred_element_type=jnp.float32)
        back = jnp.concatenate(
            [
                found[:, (r * fsdp + f) * unit : (r * fsdp + f + 1) * unit]
                for f in range(fsdp)
                for r in range(replica)
            ],
            axis=1,
        )
        values = hidden[inside].astype(jnp.float32).reshape(tokens * top, width)
        scaled = route_column(turned[1, at]) * back
        hidden_grad[inside] = scaled.reshape(tokens, top, width).astype(jnp.bfloat16)
        column = jnp.sum(values * back, axis=1, keepdims=True)
        gate_turned[at] = route_square(column, tokens, top)

    @pl.when(pl.program_id(0) == pl.num_programs(0) - 1)
    def _():
        gate_grad[...] = gate_turned[...].T


def scale_kernel(place, values, exponents, out, scales):
    _, unit, model_width = values.shape
    blocks = exponents.shape[1]
    width = model_width // blocks
    scales[...] = jnp.exp2(exponents[0].astype(jnp.float32)).T
    rows = scales[pl.ds(pl.multiple_of(place[2] * unit, unit), unit), :]
    for b in range(blocks):
        at = slice(b * width, (b + 1) * width)
        out[0, :, at] = (values[0, :, at].astype(jnp.float32) * rows[:, b : b + 1]).astype(
            jnp.bfloat16
        )


def back_kernel(parts, place, dy, *refs):
    fsdp = parts[0]
    weights, out, rows = refs[:fsdp], refs[-2], refs[-1]
    here, unit, _ = weights[0].shape

    @pl.when(pl.program_id(0) == 0)
    def _():
        for e in range(here):
            for o in range(fsdp):
                at = (e * fsdp + lax.rem(place[1] + o, fsdp)) * unit
                rows[pl.ds(pl.multiple_of(at, unit), unit), :] = weights[o][e]

    back = lax.dot_general(
        dy[...], rows[...], (((1,), (1,)), ((), ())), preferred_element_type=jnp.float32
    )
    out[...] = back.astype(jnp.bfloat16).reshape(out.shape)


def gradient_kernel(parts, place, *refs):
    fsdp, replica = parts
    hids, dys, outs, turned = (
        refs[:replica],
        refs[replica : 2 * replica],
        refs[2 * replica : -1],
        refs[-1],
    )
    here, unit, _ = outs[0].shape

    @pl.when(pl.program_id(0) == 0)
    def _():
        for c in range(replica):
            turned[c] = hids[c][...].reshape(turned.shape[2], turned.shape[1]).T

    total = sum(
        jnp.dot(turned[c], dys[c][...], preferred_element_type=jnp.float32)
        for c in range(replica)
    )
    for e in range(here):
        for o in range(fsdp):
            at = (e * fsdp + o) * unit
            outs[o][e] = total[at : at + unit].astype(outs[o].dtype)


def dense_body(
    out_grad, hidden_saved, gate_probs, expert_ids, weight_q, weight_exp, master, moment1, moment2
):
    tokens, top = expert_ids.shape
    here, rows_here, model_width = weight_q.shape
    width = hidden_saved.shape[2]
    halves, line, pair = lax.axis_size("half"), lax.axis_size("line"), lax.axis_size("pair")
    groups = halves * line * pair
    fsdp, replica = lax.axis_size("fsdp"), lax.axis_size("replica")
    place_of = {name: lax.axis_index(name) for name in ("half", "line", "pair")}
    mf, mr = lax.axis_index("fsdp"), lax.axis_index("replica")
    unit = width // (fsdp * replica)
    block = min(TOKEN_BLOCK * PARTS, tokens)
    lanes = here * fsdp * unit

    def shift(x, axis, by, across=0):
        size = lax.axis_size(axis)
        if not across:
            return lax.ppermute(x, axis, [(i, (i + by) % size) for i in range(size)])
        pairs = [
            (i * pair + j, (i + by) % size * pair + (j + across) % pair)
            for i in range(size)
            for j in range(pair)
        ]
        return lax.ppermute(x, (axis, "pair"), pairs)

    def source_of(b, i, j):
        place = 0
        for name, by in (("half", b), ("line", i), ("pair", j)):
            size = lax.axis_size(name)
            place = place * size + lax.rem(place_of[name] + (size - by), size)
        return place

    def exchange(x):
        x = x.reshape(replica * groups, tokens, lanes)
        x = lax.all_to_all(x, ("replica", "half", "line", "pair"), split_axis=0, concat_axis=0, tiled=True)
        return x.reshape(replica, groups, tokens, lanes)

    place = jnp.stack([mf, mf, mr]).astype(jnp.int32)
    weight_part = pl.pallas_call(
        scale_kernel,
        out_shape=jax.ShapeDtypeStruct((here, unit, model_width), jnp.bfloat16),
        grid_spec=pltpu.PrefetchScalarGridSpec(
            num_scalar_prefetch=1,
            grid=(here,),
            in_specs=[
                pl.BlockSpec((1, unit, model_width), lambda e, p: (e, p[2], 0)),
                pl.BlockSpec((1, weight_exp.shape[2], rows_here), lambda e, p: (e, 0, 0)),
            ],
            out_specs=pl.BlockSpec((1, unit, model_width), lambda e, p: (e, 0, 0)),
            scratch_shapes=[pltpu.VMEM((rows_here, weight_exp.shape[2]), jnp.float32)],
        ),
        compiler_params=pltpu.CompilerParams(vmem_limit_bytes=20 * 2**20),
        name="scale",
    )(place, weight_q, weight_exp.swapaxes(1, 2))

    token_specs = [
        pl.BlockSpec((top, tokens), lambda i, p: (0, 0)),
        pl.BlockSpec((top, tokens), lambda i, p: (0, 0)),
        pl.BlockSpec((block, top, width), lambda i, p: (i, 0, 0)),
    ]
    turned = pltpu.VMEM((2, tokens, top), jnp.float32)
    row_spec = pl.BlockSpec((replica, groups, block, lanes), lambda i, p: (0, 0, i, 0))
    spread = pl.pallas_call(
        lambda *refs: spread_kernel(here, (fsdp, replica), *refs),
        out_shape=jax.ShapeDtypeStruct((replica, groups, tokens, lanes), jnp.bfloat16),
        grid_spec=pltpu.PrefetchScalarGridSpec(
            num_scalar_prefetch=1,
            grid=(tokens // block,),
            in_specs=token_specs,
            out_specs=row_spec,
            scratch_shapes=[turned],
        ),
        compiler_params=pltpu.CompilerParams(vmem_limit_bytes=20 * 2**20),
        name="spread",
    )(place, expert_ids.T, gate_probs.T, hidden_saved)

    dy = {(0, 0, 0): out_grad}
    for b in range(1, halves):
        dy[b, 0, 0] = shift(out_grad, "half", b)
    after, weight_part = lax.optimization_barrier((out_grad, weight_part))
    for i in range(1, line):
        dy[0, i, 0] = shift(after, "line", i)
    for j in range(1, pair):
        dy[0, 0, j] = shift(after, "pair", j)
    keys = [key for key in sorted(dy, reverse=True) if not key[1]]
    held = lax.optimization_barrier([dy[key] for key in keys] + [spread])
    spread = held[-1]
    dy.update(zip(keys, held))
    hid = exchange(spread)
    for b in range(1, halves):
        for i in range(1, line):
            dy[b, i, 0] = shift(dy[b, 0, 0], "line", i)
    weight_parts = [weight_part] + [
        lax.ppermute(weight_part, "fsdp", [(f, (f - o) % fsdp) for f in range(fsdp)])
        for o in range(1, fsdp)
    ]
    own = jnp.zeros((groups, tokens, model_width), jnp.bfloat16)
    for b in range(halves):
        for i in range(line):
            for j in range(pair):
                if (b, i, j) not in dy:
                    dy[b, i, j] = (shift(dy[b, 0, 0], "line", i, j) if i else shift(dy[b, 0, 0], "pair", j)) if b else shift(dy[0, i, 0], "pair", j)
                own = lax.dynamic_update_index_in_dim(own, dy[b, i, j], source_of(b, i, j), 0)
    own, weight_parts = lax.optimization_barrier(
        (own.reshape(groups * tokens, model_width), weight_parts)
    )
    dy = [own] + [
        lax.ppermute(own, "replica", [(r, (r - c) % replica) for r in range(replica)])
        for c in range(1, replica)
    ]

    together = max(g for g in (1, 2, 4) if groups % g == 0)
    part_spec = pl.BlockSpec((here, unit, model_width), lambda i, p: (0, 0, 0))
    back = []
    for c in range(replica):
        back = [
            pl.pallas_call(
                lambda *refs: back_kernel((fsdp, replica), *refs),
                out_shape=jax.ShapeDtypeStruct((replica, groups, tokens, lanes), jnp.bfloat16),
                grid_spec=pltpu.PrefetchScalarGridSpec(
                    num_scalar_prefetch=1,
                    grid=(groups // together,),
                    in_specs=[
                        pl.BlockSpec((together * tokens, model_width), lambda i, p: (i, 0))
                    ]
                    + [part_spec] * fsdp
                    + [pl.BlockSpec(memory_space=pl.ANY)] * len(back),
                    out_specs=pl.BlockSpec(
                        (1, together, tokens, lanes),
                        lambda i, p, c=c: (lax.rem(p[2] + c, replica), i, 0, 0),
                    ),
                    scratch_shapes=[pltpu.VMEM((lanes, model_width), jnp.bfloat16)],
                ),
                compiler_params=pltpu.CompilerParams(vmem_limit_bytes=36 * 2**20),
                cost_estimate=pl.CostEstimate(
                    flops=2 * groups * tokens * lanes * model_width,
                    bytes_accessed=2 * groups * tokens * (lanes + model_width),
                    transcendentals=0,
                ),
                input_output_aliases={2 + fsdp: 0} if back else {},
                name="back",
            )(place, dy[c], *weight_parts, *back)
        ]
    back, hid = lax.optimization_barrier((back[0], hid))
    returned = exchange(back)

    columns = min(512, model_width)
    grad_spec = pl.BlockSpec((here, unit, columns), lambda i, p: (0, 0, i))
    grads = pl.pallas_call(
        lambda *refs: gradient_kernel((fsdp, replica), *refs),
        out_shape=[
            jax.ShapeDtypeStruct((here, unit, model_width), jnp.bfloat16 if o else jnp.float32)
            for o in range(fsdp)
        ],
        grid_spec=pltpu.PrefetchScalarGridSpec(
            num_scalar_prefetch=1,
            grid=(model_width // columns,),
            in_specs=[
                pl.BlockSpec(
                    (1, groups, tokens, lanes),
                    lambda i, p, c=c: (lax.rem(p[2] + c, replica), 0, 0, 0),
                )
                for c in range(replica)
            ]
            + [pl.BlockSpec((groups * tokens, columns), lambda i, p: (0, i))] * replica,
            out_specs=[grad_spec] * fsdp,
            scratch_shapes=[pltpu.VMEM((replica, lanes, groups * tokens), jnp.bfloat16)],
        ),
        compiler_params=pltpu.CompilerParams(vmem_limit_bytes=20 * 2**20),
        cost_estimate=pl.CostEstimate(
            flops=2 * replica * groups * tokens * lanes * model_width,
            bytes_accessed=2 * replica * groups * tokens * (lanes + model_width),
            transcendentals=0,
        ),
        name="gradient",
    )(place, *[hid] * replica, *dy)
    gradient = grads[0]
    for o in range(1, fsdp):
        gradient = gradient + lax.ppermute(
            grads[o], "fsdp", [(f, (f + o) % fsdp) for f in range(fsdp)]
        ).astype(jnp.float32)
    first = 0.9 * moment1.astype(jnp.float32) + 0.1 * gradient
    second = 0.95 * moment2.astype(jnp.float32) + 0.05 * gradient * gradient
    update = first / (1.0 - 0.9**20) / (jnp.sqrt(second / (1.0 - 0.95**20)) + 1e-08) + 0.1 * master
    master_new = master - 0.001 * update

    new = (master_new, first.astype(jnp.bfloat16), second.astype(jnp.bfloat16))
    returned, new = lax.optimization_barrier((returned, new))
    hidden_grad, gate_grad = pl.pallas_call(
        lambda *refs: collect_kernel(here, (fsdp, replica), *refs),
        out_shape=[
            jax.ShapeDtypeStruct(hidden_saved.shape, jnp.bfloat16),
            jax.ShapeDtypeStruct((top, tokens), jnp.float32),
        ],
        grid=(tokens // block,),
        in_specs=[
            pl.BlockSpec((top, tokens), lambda i: (0, 0)),
            pl.BlockSpec((top, tokens), lambda i: (0, 0)),
            pl.BlockSpec((block, top, width), lambda i: (i, 0, 0)),
            pl.BlockSpec((replica, groups, block, lanes), lambda i: (0, 0, i, 0)),
        ],
        out_specs=[
            pl.BlockSpec((block, top, width), lambda i: (i, 0, 0)),
            pl.BlockSpec((top, tokens), lambda i: (0, 0)),
        ],
        scratch_shapes=[turned, pltpu.VMEM((tokens, top), jnp.float32)],
        compiler_params=pltpu.CompilerParams(vmem_limit_bytes=20 * 2**20),
        name="collect",
    )(
        expert_ids.T,
        gate_probs.T,
        pltpu.with_memory_space_constraint(hidden_saved, pltpu.HBM),
        returned,
    )
    return (hidden_grad, gate_grad.T) + new


def solution(mesh):
    sizes = dict(mesh.shape)
    devices = mesh.devices.size
    groups = sizes["expert"]

    def mapped(function, mesh, expert):
        rows = P(expert + ("fsdp", "replica"))
        state = P(expert, ("fsdp", "replica"))
        weights = P(expert, "fsdp")
        in_specs = (rows,) * 4 + (weights,) * 2 + (state,) * 3
        out_specs = (rows,) * 2 + (state,) * 3
        return jax.shard_map(
            function, mesh=mesh, in_specs=in_specs, out_specs=out_specs, check_vma=False
        )

    def program(*args):
        tokens, top = args[3].shape[0] // devices, args[3].shape[1]
        dense = min(tokens, 2 * tokens * top // args[4].shape[0]) == tokens
        if not dense or groups % 4 or mesh.axis_names[0] != "expert":
            return mapped(slots_body, mesh, ("expert",))(*args)
        halves = jax.sharding.Mesh(
            mesh.devices.reshape((2, groups // 4, 2) + mesh.devices.shape[1:]),
            ("half", "line", "pair") + mesh.axis_names[1:],
        )
        return mapped(dense_body, halves, ("half", "line", "pair"))(*args)

    return program
```

```python
import jax
import jax.numpy as jnp
from jax import lax
from jax.experimental import pallas as pl
from jax.experimental.pallas import tpu as pltpu
from jax.sharding import PartitionSpec as P

def slots_body(
    out_grad, hidden_saved, gate_probs, expert_ids, weight_q, weight_exp, master, moment1, moment2
):
    tokens_here, top_count = expert_ids.shape
    experts_here, rows_here, model_width = weight_q.shape
    hidden_width = hidden_saved.shape[2]
    expert_groups = lax.axis_size("expert")
    experts_all = expert_groups * experts_here
    capacity = min(tokens_here, 2 * tokens_here * top_count // experts_all)
    routes = tokens_here * top_count
    flat_ids = expert_ids.reshape(-1)
    onehot = (flat_ids[:, None] == jnp.arange(experts_all, dtype=jnp.int32)[None, :]).astype(
        jnp.int32
    )
    rank_in_expert = jnp.sum(jnp.cumsum(onehot, axis=0) * onehot, axis=1) - 1
    slot_index = flat_ids * capacity + rank_in_expert
    route_of_slot = (
        jnp.full((experts_all * capacity,), routes, jnp.int32)
        .at[slot_index]
        .set(jnp.arange(routes, dtype=jnp.int32))
    )
    filled = route_of_slot < routes
    clamped = jnp.minimum(route_of_slot, routes - 1)
    weighted = (
        (gate_probs[..., None] * hidden_saved.astype(jnp.float32))
        .astype(jnp.bfloat16)
        .reshape(routes, hidden_width)
    )
    zero_value = jnp.zeros((), jnp.bfloat16)
    dy_send = jnp.where(filled[:, None], out_grad[clamped // top_count], zero_value)
    weighted_send = jnp.where(filled[:, None], weighted[clamped], zero_value)
    dy_send = dy_send.reshape(expert_groups, experts_here, capacity, model_width)
    weighted_send = weighted_send.reshape(expert_groups, experts_here, capacity, hidden_width)
    recv_dy, recv_weighted = (
        lax.all_to_all(dy_send, "expert", split_axis=0, concat_axis=0, tiled=True),
        lax.all_to_all(weighted_send, "expert", split_axis=0, concat_axis=0, tiled=True),
    )
    scales = jnp.exp2(weight_exp.astype(jnp.float32))
    blocks = weight_exp.shape[2]
    weight_local = (
        (
            weight_q.astype(jnp.float32).reshape(
                experts_here, rows_here, blocks, model_width // blocks
            )
            * scales[..., None]
        )
        .reshape(experts_here, rows_here, model_width)
        .astype(jnp.bfloat16)
    )
    back_rows = jnp.einsum(
        "secd,efd->secf",
        recv_dy,
        lax.all_gather(weight_local, "fsdp", axis=1, tiled=True),
        preferred_element_type=jnp.float32,
    ).astype(jnp.bfloat16)
    returned = lax.all_to_all(back_rows, "expert", split_axis=0, concat_axis=0, tiled=True)
    back_route = returned.reshape(experts_all * capacity, hidden_width)[slot_index].reshape(
        tokens_here, top_count, hidden_width
    )
    back_float = back_route.astype(jnp.float32)
    hidden_grad = (gate_probs[..., None] * back_float).astype(jnp.bfloat16)
    gate_grad = jnp.sum(hidden_saved.astype(jnp.float32) * back_float, axis=-1)
    partial_grad = jnp.einsum(
        "secf,secd->efd", recv_weighted, recv_dy, preferred_element_type=jnp.float32
    )
    gradient = lax.psum_scatter(partial_grad, ("fsdp", "replica"), scatter_dimension=1, tiled=True)
    first = 0.9 * moment1.astype(jnp.float32) + 0.1 * gradient
    second = 0.95 * moment2.astype(jnp.float32) + 0.05 * gradient * gradient
    update = first / (1.0 - 0.9**20) / (jnp.sqrt(second / (1.0 - 0.95**20)) + 1e-08) + 0.1 * master
    master_new = master - 0.001 * update
    return (
        hidden_grad,
        gate_grad,
        master_new,
        first.astype(jnp.bfloat16),
        second.astype(jnp.bfloat16),
    )


VMEM = 100 * 2**20 // 2
TOKEN_BLOCK = 16
PARTS = 4


def pick(index, options):
    result = options[0]
    for number, option in enumerate(options[1:], 1):
        result = jnp.where(index == number, option, result)
    return result


def diagonal(shape):
    return lax.broadcasted_iota(jnp.int32, shape, 1) == lax.broadcasted_iota(jnp.int32, shape, 2)


def route_column(values):
    tokens, top = values.shape
    shape = (tokens, top, top)
    spread = jnp.where(diagonal(shape), jnp.broadcast_to(values[:, None, :], shape), 0.0)
    return jnp.sum(spread.reshape(tokens * top, top), axis=1, keepdims=True)


def route_square(column, tokens, top):
    shape = (tokens, top, top)
    spread = jnp.broadcast_to(column, (tokens * top, top)).reshape(shape)
    return jnp.sum(jnp.where(diagonal(shape), spread, 0.0), axis=1)


def route_match(ids, experts):
    tokens, top = ids.shape
    token = lax.broadcasted_iota(jnp.int32, (tokens, top), 0).astype(jnp.float32)
    keys = route_column(ids * tokens + token).astype(jnp.int32)
    columns = lax.broadcasted_iota(jnp.int32, (tokens * top, experts * tokens), 1)
    return jnp.where(keys == columns, 1.0, 0.0).astype(jnp.bfloat16)


def turn_routes(ids, gate, turned):
    @pl.when(pl.program_id(0) == 0)
    def _():
        turned[0] = ids[...].astype(jnp.float32).T
        turned[1] = gate[...].T


def rows_of_part(step, part, tokens):
    start = pl.program_id(0) * step + part * tokens
    return pl.ds(pl.multiple_of(start, tokens), tokens)


def spread_kernel(here, parts, place, ids, gate, hidden, out, turned):
    fsdp, replica = parts
    step, top, width = hidden.shape
    tokens = min(TOKEN_BLOCK, step)
    groups = out.shape[1]
    unit = width // (fsdp * replica)
    turn_routes(ids, gate, turned)
    for part in range(step // tokens):
        inside = slice(part * tokens, (part + 1) * tokens)
        at = rows_of_part(step, part, tokens)
        match = route_match(turned[0, at], groups * here)
        values = hidden[inside].astype(jnp.float32).reshape(tokens * top, width)
        weighted = (route_column(turned[1, at]) * values).astype(jnp.bfloat16)
        for r in range(replica):
            blocks = [
                weighted[:, (f * replica + r) * unit : (f * replica + r + 1) * unit]
                for f in range(fsdp)
            ]
            share = pick(
                place[1],
                [jnp.concatenate(blocks[f:] + blocks[:f], axis=1) for f in range(fsdp)],
            )
            rows = lax.dot_general(
                match, share, (((0,), (0,)), ((), ())), preferred_element_type=jnp.float32
            ).astype(jnp.bfloat16)
            for g in range(groups):
                for e in range(here):
                    row = (g * here + e) * tokens
                    out[r, g, inside, e * fsdp * unit : (e + 1) * fsdp * unit] = rows[
                        row : row + tokens
                    ]


def collect_kernel(
    here, parts, ids, gate, hidden, backs, hidden_grad, gate_grad, turned, gate_turned, held, sems
):
    fsdp, replica = parts
    step, top, width = hidden_grad.shape
    tokens = min(TOKEN_BLOCK, step)
    groups = backs.shape[1]
    unit = width // (fsdp * replica)

    def fetch(number):
        rows = pl.ds(pl.multiple_of(number * step, step), step)
        return pltpu.make_async_copy(hidden.at[rows], held.at[rows], sems.at[number])

    @pl.when(pl.program_id(0) == 0)
    def _():
        for number in range(held.shape[0] // step):
            fetch(number).start()

    turn_routes(ids, gate, turned)
    for part in range(step // tokens):
        inside = slice(part * tokens, (part + 1) * tokens)
        at = rows_of_part(step, part, tokens)
        match = route_match(turned[0, at], groups * here)
        rows = jnp.concatenate(
            [
                jnp.concatenate(
                    [
                        backs[r, g, inside, e * fsdp * unit : (e + 1) * fsdp * unit]
                        for r in range(replica)
                    ],
                    axis=1,
                )
                for g in range(groups)
                for e in range(here)
            ],
            axis=0,
        )
        found = jnp.dot(match, rows, preferred_element_type=jnp.float32)
        back = jnp.concatenate(
            [
                found[:, (r * fsdp + f) * unit : (r * fsdp + f + 1) * unit]
                for f in range(fsdp)
                for r in range(replica)
            ],
            axis=1,
        )
        scaled = route_column(turned[1, at]) * back
        hidden_grad[inside] = scaled.reshape(tokens, top, width).astype(jnp.bfloat16)
        if part == 0:
            fetch(pl.program_id(0)).wait()
        values = held[at].astype(jnp.float32).reshape(tokens * top, width)
        column = jnp.sum(values * back, axis=1, keepdims=True)
        gate_turned[at] = route_square(column, tokens, top)

    @pl.when(pl.program_id(0) == pl.num_programs(0) - 1)
    def _():
        gate_grad[...] = gate_turned[...].T


def scale_kernel(place, values, exponents, out, scales):
    _, unit, model_width = values.shape
    blocks = exponents.shape[1]
    width = model_width // blocks
    scales[...] = jnp.exp2(exponents[0].astype(jnp.float32)).T
    rows = scales[pl.ds(pl.multiple_of(place[2] * unit, unit), unit), :]
    for b in range(blocks):
        at = slice(b * width, (b + 1) * width)
        out[0, :, at] = (values[0, :, at].astype(jnp.float32) * rows[:, b : b + 1]).astype(
            jnp.bfloat16
        )


def back_kernel(parts, place, dy, *refs):
    fsdp = parts[0]
    weights, out, rows = refs[:fsdp], refs[-2], refs[-1]
    here, unit, _ = weights[0].shape

    @pl.when(pl.program_id(0) == 0)
    def _():
        for e in range(here):
            for o in range(fsdp):
                at = (e * fsdp + lax.rem(place[1] + o, fsdp)) * unit
                rows[pl.ds(pl.multiple_of(at, unit), unit), :] = weights[o][e]

    back = lax.dot_general(
        dy[...], rows[...], (((1,), (1,)), ((), ())), preferred_element_type=jnp.float32
    )
    out[...] = back.astype(jnp.bfloat16).reshape(out.shape)


def gradient_kernel(parts, place, *refs):
    fsdp, replica = parts
    hids, dys, outs, turned = (
        refs[:replica],
        refs[replica : 2 * replica],
        refs[2 * replica : -1],
        refs[-1],
    )
    here, unit, _ = outs[0].shape

    @pl.when(pl.program_id(0) == 0)
    def _():
        for c in range(replica):
            turned[c] = hids[c][...].reshape(turned.shape[2], turned.shape[1]).T

    total = sum(
        jnp.dot(turned[c], dys[c][...], preferred_element_type=jnp.float32)
        for c in range(replica)
    )
    for e in range(here):
        for o in range(fsdp):
            at = (e * fsdp + o) * unit
            outs[o][e] = total[at : at + unit].astype(outs[o].dtype)


def dense_body(
    out_grad, hidden_saved, gate_probs, expert_ids, weight_q, weight_exp, master, moment1, moment2
):
    tokens, top = expert_ids.shape
    here, rows_here, model_width = weight_q.shape
    width = hidden_saved.shape[2]
    halves, line, pair = lax.axis_size("half"), lax.axis_size("line"), lax.axis_size("pair")
    groups = halves * line * pair
    fsdp, replica = lax.axis_size("fsdp"), lax.axis_size("replica")
    place_of = {name: lax.axis_index(name) for name in ("half", "line", "pair")}
    mf, mr = lax.axis_index("fsdp"), lax.axis_index("replica")
    unit = width // (fsdp * replica)
    block = min(TOKEN_BLOCK * PARTS, tokens)
    lanes = here * fsdp * unit

    def shift(x, axis, by, across=0):
        size = lax.axis_size(axis)
        if not across:
            return lax.ppermute(x, axis, [(i, (i + by) % size) for i in range(size)])
        pairs = [
            (i * pair + j, (i + by) % size * pair + (j + across) % pair)
            for i in range(size)
            for j in range(pair)
        ]
        return lax.ppermute(x, (axis, "pair"), pairs)

    def source_of(b, i, j):
        place = 0
        for name, by in (("half", b), ("line", i), ("pair", j)):
            size = lax.axis_size(name)
            place = place * size + lax.rem(place_of[name] + (size - by), size)
        return place

    def exchange(x):
        x = x.reshape(replica * groups, tokens, lanes)
        x = lax.all_to_all(x, ("replica", "half", "line", "pair"), split_axis=0, concat_axis=0, tiled=True)
        return x.reshape(replica, groups, tokens, lanes)

    place = jnp.stack([mf, mf, mr]).astype(jnp.int32)
    weight_part = pl.pallas_call(
        scale_kernel,
        out_shape=jax.ShapeDtypeStruct((here, unit, model_width), jnp.bfloat16),
        grid_spec=pltpu.PrefetchScalarGridSpec(
            num_scalar_prefetch=1,
            grid=(here,),
            in_specs=[
                pl.BlockSpec((1, unit, model_width), lambda e, p: (e, p[2], 0)),
                pl.BlockSpec((1, weight_exp.shape[2], rows_here), lambda e, p: (e, 0, 0)),
            ],
            out_specs=pl.BlockSpec((1, unit, model_width), lambda e, p: (e, 0, 0)),
            scratch_shapes=[pltpu.VMEM((rows_here, weight_exp.shape[2]), jnp.float32)],
        ),
        compiler_params=pltpu.CompilerParams(vmem_limit_bytes=20 * 2**20),
        name="scale",
    )(place, weight_q, weight_exp.swapaxes(1, 2))

    token_specs = [
        pl.BlockSpec((top, tokens), lambda i, p: (0, 0)),
        pl.BlockSpec((top, tokens), lambda i, p: (0, 0)),
        pl.BlockSpec((block, top, width), lambda i, p: (i, 0, 0)),
    ]
    turned = pltpu.VMEM((2, tokens, top), jnp.float32)
    row_spec = pl.BlockSpec((replica, groups, block, lanes), lambda i, p: (0, 0, i, 0))
    spread = pl.pallas_call(
        lambda *refs: spread_kernel(here, (fsdp, replica), *refs),
        out_shape=jax.ShapeDtypeStruct((replica, groups, tokens, lanes), jnp.bfloat16),
        grid_spec=pltpu.PrefetchScalarGridSpec(
            num_scalar_prefetch=1,
            grid=(tokens // block,),
            in_specs=token_specs,
            out_specs=row_spec,
            scratch_shapes=[turned],
        ),
        compiler_params=pltpu.CompilerParams(vmem_limit_bytes=20 * 2**20),
        name="spread",
    )(place, expert_ids.T, gate_probs.T, hidden_saved)

    dy = {(0, 0, 0): out_grad}
    for b in range(1, halves):
        dy[b, 0, 0] = shift(out_grad, "half", b)
    after, weight_part = lax.optimization_barrier((out_grad, weight_part))
    for i in range(1, line):
        dy[0, i, 0] = shift(after, "line", i)
    for j in range(1, pair):
        dy[0, 0, j] = shift(after, "pair", j)
    keys = [key for key in sorted(dy, reverse=True) if not key[1]]
    held = lax.optimization_barrier([dy[key] for key in keys] + [spread])
    spread = held[-1]
    dy.update(zip(keys, held))
    hid = exchange(spread)
    for b in range(1, halves):
        for i in range(1, line):
            dy[b, i, 0] = shift(dy[b, 0, 0], "line", i)
    weight_parts = [weight_part] + [
        lax.ppermute(weight_part, "fsdp", [(f, (f - o) % fsdp) for f in range(fsdp)])
        for o in range(1, fsdp)
    ]
    own = jnp.zeros((groups, tokens, model_width), jnp.bfloat16)
    for b in range(halves):
        for i in range(line):
            for j in range(pair):
                if (b, i, j) not in dy:
                    dy[b, i, j] = (shift(dy[b, 0, 0], "line", i, j) if i else shift(dy[b, 0, 0], "pair", j)) if b else shift(dy[0, i, 0], "pair", j)
                own = lax.dynamic_update_index_in_dim(own, dy[b, i, j], source_of(b, i, j), 0)
    own, weight_parts = lax.optimization_barrier(
        (own.reshape(groups * tokens, model_width), weight_parts)
    )
    dy = [own] + [
        lax.ppermute(own, "replica", [(r, (r - c) % replica) for r in range(replica)])
        for c in range(1, replica)
    ]

    together = max(g for g in (1, 2, 4) if groups % g == 0)
    part_spec = pl.BlockSpec((here, unit, model_width), lambda i, p: (0, 0, 0))
    back = []
    for c in range(replica):
        back = [
            pl.pallas_call(
                lambda *refs: back_kernel((fsdp, replica), *refs),
                out_shape=jax.ShapeDtypeStruct((replica, groups, tokens, lanes), jnp.bfloat16),
                grid_spec=pltpu.PrefetchScalarGridSpec(
                    num_scalar_prefetch=1,
                    grid=(groups // together,),
                    in_specs=[
                        pl.BlockSpec((together * tokens, model_width), lambda i, p: (i, 0))
                    ]
                    + [part_spec] * fsdp
                    + [pl.BlockSpec(memory_space=pl.ANY)] * len(back),
                    out_specs=pl.BlockSpec(
                        (1, together, tokens, lanes),
                        lambda i, p, c=c: (lax.rem(p[2] + c, replica), i, 0, 0),
                    ),
                    scratch_shapes=[pltpu.VMEM((lanes, model_width), jnp.bfloat16)],
                ),
                compiler_params=pltpu.CompilerParams(vmem_limit_bytes=36 * 2**20),
                cost_estimate=pl.CostEstimate(
                    flops=2 * groups * tokens * lanes * model_width,
                    bytes_accessed=2 * groups * tokens * (lanes + model_width),
                    transcendentals=0,
                ),
                input_output_aliases={2 + fsdp: 0} if back else {},
                name="back",
            )(place, dy[c], *weight_parts, *back)
        ]
    back, hid = lax.optimization_barrier((back[0], hid))
    returned = exchange(back)

    columns = min(512, model_width)
    grad_spec = pl.BlockSpec((here, unit, columns), lambda i, p: (0, 0, i))
    grads = pl.pallas_call(
        lambda *refs: gradient_kernel((fsdp, replica), *refs),
        out_shape=[
            jax.ShapeDtypeStruct((here, unit, model_width), jnp.bfloat16 if o else jnp.float32)
            for o in range(fsdp)
        ],
        grid_spec=pltpu.PrefetchScalarGridSpec(
            num_scalar_prefetch=1,
            grid=(model_width // columns,),
            in_specs=[
                pl.BlockSpec(
                    (1, groups, tokens, lanes),
                    lambda i, p, c=c: (lax.rem(p[2] + c, replica), 0, 0, 0),
                )
                for c in range(replica)
            ]
            + [pl.BlockSpec((groups * tokens, columns), lambda i, p: (0, i))] * replica,
            out_specs=[grad_spec] * fsdp,
            scratch_shapes=[pltpu.VMEM((replica, lanes, groups * tokens), jnp.bfloat16)],
        ),
        compiler_params=pltpu.CompilerParams(vmem_limit_bytes=20 * 2**20),
        cost_estimate=pl.CostEstimate(
            flops=2 * replica * groups * tokens * lanes * model_width,
            bytes_accessed=2 * replica * groups * tokens * (lanes + model_width),
            transcendentals=0,
        ),
        name="gradient",
    )(place, *[hid] * replica, *dy)
    gradient = grads[0]
    for o in range(1, fsdp):
        gradient = gradient + lax.ppermute(
            grads[o], "fsdp", [(f, (f + o) % fsdp) for f in range(fsdp)]
        ).astype(jnp.float32)
    first = 0.9 * moment1.astype(jnp.float32) + 0.1 * gradient
    second = 0.95 * moment2.astype(jnp.float32) + 0.05 * gradient * gradient
    update = first / (1.0 - 0.9**20) / (jnp.sqrt(second / (1.0 - 0.95**20)) + 1e-08) + 0.1 * master
    master_new = master - 0.001 * update

    new = (master_new, first.astype(jnp.bfloat16), second.astype(jnp.bfloat16))
    returned, new = lax.optimization_barrier((returned, new))
    hidden_grad, gate_grad = pl.pallas_call(
        lambda *refs: collect_kernel(here, (fsdp, replica), *refs),
        out_shape=[
            jax.ShapeDtypeStruct(hidden_saved.shape, jnp.bfloat16),
            jax.ShapeDtypeStruct((top, tokens), jnp.float32),
        ],
        grid=(tokens // block,),
        in_specs=[
            pl.BlockSpec((top, tokens), lambda i: (0, 0)),
            pl.BlockSpec((top, tokens), lambda i: (0, 0)),
            pl.BlockSpec(memory_space=pltpu.HBM),
            pl.BlockSpec((replica, groups, block, lanes), lambda i: (0, 0, i, 0)),
        ],
        out_specs=[
            pl.BlockSpec((block, top, width), lambda i: (i, 0, 0)),
            pl.BlockSpec((top, tokens), lambda i: (0, 0)),
        ],
        scratch_shapes=[
            turned,
            pltpu.VMEM((tokens, top), jnp.float32),
            pltpu.VMEM(hidden_saved.shape, jnp.bfloat16),
            pltpu.SemaphoreType.DMA((tokens // block,)),
        ],
        compiler_params=pltpu.CompilerParams(vmem_limit_bytes=20 * 2**20),
        name="collect",
    )(
        expert_ids.T,
        gate_probs.T,
        pltpu.with_memory_space_constraint(hidden_saved, pltpu.HBM),
        returned,
    )
    return (hidden_grad, gate_grad.T) + new


def solution(mesh):
    sizes = dict(mesh.shape)
    devices = mesh.devices.size
    groups = sizes["expert"]

    def mapped(function, mesh, expert):
        rows = P(expert + ("fsdp", "replica"))
        state = P(expert, ("fsdp", "replica"))
        weights = P(expert, "fsdp")
        in_specs = (rows,) * 4 + (weights,) * 2 + (state,) * 3
        out_specs = (rows,) * 2 + (state,) * 3
        return jax.shard_map(
            function, mesh=mesh, in_specs=in_specs, out_specs=out_specs, check_vma=False
        )

    def program(*args):
        tokens, top = args[3].shape[0] // devices, args[3].shape[1]
        dense = min(tokens, 2 * tokens * top // args[4].shape[0]) == tokens
        if not dense or groups % 4 or mesh.axis_names[0] != "expert":
            return mapped(slots_body, mesh, ("expert",))(*args)
        halves = jax.sharding.Mesh(
            mesh.devices.reshape((2, groups // 4, 2) + mesh.devices.shape[1:]),
            ("half", "line", "pair") + mesh.axis_names[1:],
        )
        return mapped(dense_body, halves, ("half", "line", "pair"))(*args)

    return program
```
